128 devices in a mesh: kpair: 32 (over z, x, core), vir: 4 (over y).
Axes of the slice: x: 4, y: 4, z: 4, core: 2. Of those that a mesh axis runs over, the one named last changes fastest.
Arguments:
- lam: bfloat16 [32, 256, 9216], P('kpair', None, 'vir'), may hold values from -6 to 6
- chol: bfloat16 [32, 384, 9216], P('kpair', None, 'vir'), may hold values from -0.3125 to 0.3125
- cycle_int: bfloat16 [32, 1536, 1536], P('kpair', 'vir'), may hold values from -0.15625 to 0.15625
- sources: int32 [32, 2], replicated, may hold values from 0 to 31, as said below
Outputs:
- resid: float32 [32, 256, 9216], P('kpair', None, 'vir')
The draws below stay inside these ranges and needn't reach their ends.
Inputs may be any that keep to these rules, and one draw needn't show every extreme that they name: `sources`: column 0 is a permutation of the 32 blocks; column 1 names any block, and several targets may name the same one; both columns reach 0 and 31.
All inputs are finite; a program needn't handle non-finite values.
Results may differ from the reference program's by a relative error of at most 0.0026.
Values may be sent and summed in bfloat16 or wider, within the bound.
A program may use at most 192 MiB of HBM per device.

```python
import jax
import jax.numpy as jnp
from jax import lax

O = 16
V = 96
NAUX = 384
NBLK = 32


def draw_sources(key, part):
    key = jax.random.fold_in(key, 7)
    first_key, second_key = jax.random.split(key)
    first = jax.random.permutation(first_key, NBLK).astype(jnp.int32)
    second = jax.random.randint(second_key, (NBLK,), 0, NBLK).astype(jnp.int32)
    second = second.at[0].set(0).at[NBLK - 1].set(NBLK - 1)
    return jnp.stack([first, second], axis=1).astype(jnp.int32)


def block_scale(stream_key, shape, pieces, low, high):
    def one(axis_at, parts):
        draws = jax.random.uniform(jax.random.fold_in(jax.random.fold_in(stream_key, 6), axis_at), (parts,), jnp.float32, low / len(pieces), high / len(pieces))
        return jnp.repeat(jnp.exp(draws), shape[axis_at] // parts).reshape((-1,) + (1,) * (len(shape) - axis_at - 1))

    level = one(*pieces[0])
    for cut in pieces[1:]:
        level = level * one(*cut)
    return level


def gaussian(stream_key, dims, spread, limit, pieces=(), held_as=jnp.bfloat16):
    factor_of = block_scale(stream_key, dims, pieces, -0.22, 0.18) if pieces else 1.0
    result = jax.random.normal(stream_key, dims, jnp.float32) * spread * factor_of
    return jnp.minimum(jnp.maximum(result, -limit), limit).astype(held_as)


def setup_inputs(seed: int = 0) -> dict:
    key_list = jax.random.split(jax.random.key(seed), 5)
    lam = gaussian(key_list[0], (NBLK, O * O, V * V), 1.0, 6.0, ((0, 32), (2, 4)))
    chol = gaussian(key_list[1], (NBLK, NAUX, V * V), ((V * V * NAUX) ** -0.25), 0.3125, ((0, 32), (2, 4)))
    cycle_int = gaussian(key_list[2], (NBLK, V * O, O * V), (O * V) ** -0.5, 0.15625, ((0, 32), (1, 4)))
    sources = draw_sources(jax.random.fold_in(key_list[4], 71), 0)
    return {"lam": lam, "chol": chol, "cycle_int": cycle_int, "sources": sources}


column_block = 8


def reference(lam, chol, cycle_int, sources):
    def one(target):
        ladder_src = lam[sources[target, 0]]
        cycle_src = lam[sources[target, 1]]
        factor = chol[target].astype(jnp.float32).reshape(NAUX, V, V)

        def step(turn, total):
            start = turn * column_block
            part = lax.dynamic_slice_in_dim(factor, start, column_block, 2)
            block = jnp.einsum("qac,qbd->cdab", part, factor).astype(jnp.bfloat16)
            block = block.reshape(column_block * V, V * V)
            rows = lax.dynamic_slice_in_dim(ladder_src, start * V, column_block * V, 1)
            return total + jnp.dot(rows, block, preferred_element_type=jnp.float32)

        ladder = lax.fori_loop(0, V // column_block, step, jnp.zeros((O * O, V * V), jnp.float32))
        left = cycle_src.astype(jnp.float32).reshape(O, O, V, V)
        right = cycle_int[target].astype(jnp.float32).reshape(V, O, O, V)
        cycle = jnp.einsum("ikac,ckjb->ijab", left, right).reshape(O * O, V * V)
        return ladder + cycle

    return lax.map(one, jnp.arange(NBLK, dtype=jnp.int32))
```

```python
import functools

import jax
import jax.numpy as jnp
from jax import lax
from jax.experimental import pallas as pl
from jax.experimental.pallas import tpu as pltpu
from jax.sharding import PartitionSpec as P

O = 16
V = 96
VS = 24
NAUX = 384
OO = O * O
SLAB = VS * V
PAD = 128
BF = jnp.bfloat16
F32 = jnp.float32
MESH = pl.DeviceIdType.MESH
B_CHUNKS = 4


class Place:
    def __init__(self):
        kp = lax.axis_index("kpair")
        y = lax.axis_index("vir")
        core = kp % 2
        half = y // 2
        guest = (core + half) % 2
        other = y + 1 - 2 * (y % 2)
        swap = kp + 1 - 2 * core
        self.kp, self.y, self.half, self.guest = kp, y, half, guest
        self.home = guest == 0
        self.away = guest == 1
        self.mate = (swap, y)
        self.cross = (kp, other)
        self.partner = (swap, 3 - y)
        self.own_slab = y + guest * (3 - 2 * y)
        self.mate_slab = y + (1 - guest) * (3 - 2 * y)
        self.cross_slab = other + guest * (3 - 2 * other)
        self.diag_slab = other + (1 - guest) * (3 - 2 * other)


def remote(src, dst, send, recv, device):
    return pltpu.make_async_remote_copy(
        src_ref=src, dst_ref=dst, send_sem=send, recv_sem=recv, device_id=device, device_id_type=MESH
    )


def loop(count, body):
    def step(i, carry):
        body(i)
        return carry

    lax.fori_loop(0, count, step, 0)


def rows_of(index, size):
    return pl.ds(pl.multiple_of(index * size, size), size)


def spread_kernel(
    n, src, lam, ft, pt, lw, sw, fall, ptw, z, stage, z_send, z_recv, w_send, w_recv, b_send, b_recv, p_send, p_recv, own_sem
):
    at = Place()
    rows = 2 * OO // n
    lanes = SLAB // 2

    def piece(ref, q):
        return ref.at[rows_of(q // 2, rows), pl.ds(pl.multiple_of((q % 2) * lanes, 128), lanes)]

    barrier = pltpu.get_barrier_semaphore()

    def greet(o):
        pl.semaphore_signal(barrier, inc=1, device_id=((at.kp + o) % n, 3 - at.y), device_id_type=MESH)

    def greet_plane(o):
        pl.semaphore_signal(barrier, inc=1, device_id=((at.kp + o + 1) % n, at.y), device_id_type=MESH)

    pl.semaphore_signal(barrier, inc=1, device_id=at.cross, device_id_type=MESH)
    loop(n, greet)
    loop(n - 1, greet_plane)
    pl.semaphore_wait(barrier, 2 * n)

    def spread(o):
        q = (at.kp + o + 1) % n
        return remote(piece(lam, q), z.at[at.kp], z_send.at[q], z_recv.at[at.kp], (q, at.y))

    def spread_in(o):
        q = (at.kp + o + 1) % n
        return remote(piece(lam, at.kp), z.at[q], z_send.at[q], z_recv.at[q], (q, at.y))

    z_own = pltpu.make_async_copy(piece(lam, at.kp), z.at[at.kp], z_recv.at[at.kp])
    loop(n - 1, lambda o: spread(o).start())
    z_own.start()

    step = SLAB // B_CHUNKS

    def chunk(ref, k):
        return ref.at[pl.ds(k * step, step)]

    def b_copy(kind, src_ref, slab, k, device):
        return remote(chunk(src_ref, k), chunk(fall.at[slab], k), b_send.at[kind, k], b_recv.at[kind, k], device)

    f_own = pltpu.make_async_copy(ft, fall.at[at.own_slab], own_sem.at[0])
    p_own = pltpu.make_async_copy(pt, ptw, own_sem.at[1])
    p_swap = remote(pt, ptw, p_send, p_recv, at.partner)

    @pl.when(at.home)
    def _():
        for k in range(B_CHUNKS):
            b_copy(1, ft, at.own_slab, k, at.cross).start()
            b_copy(0, ft, at.own_slab, k, at.mate).start()
        f_own.start()
        p_own.start()

    @pl.when(at.away)
    def _():
        for k in range(B_CHUNKS):
            b_copy(3, ft, at.y, k, at.partner).start()
        p_swap.start()

    def relay(ks):
        @pl.when(at.away)
        def _():
            for k in ks:
                b_copy(3, ft, at.own_slab, k, at.partner).wait_recv()
                b_copy(1, fall.at[at.own_slab], at.own_slab, k, at.cross).start()
                b_copy(0, fall.at[at.own_slab], at.own_slab, k, at.mate).start()

    def forward(ks):
        for k in ks:
            b_copy(1, ft, at.cross_slab, k, at.cross).wait_recv()
            b_copy(2, fall.at[at.cross_slab], at.cross_slab, k, at.mate).start()

    def place(kind, t, q):
        e = t % 2
        moved = (e + at.half) % 2
        device = (t + moved * (1 - 2 * e), at.y + moved * (3 - 2 * at.y))
        out = lw if kind == 0 else sw
        return remote(stage.at[kind, t], piece(out, at.kp), w_send.at[kind, t], w_recv.at[kind, at.kp], device)

    def place_own(kind):
        out = lw if kind == 0 else sw
        return pltpu.make_async_copy(stage.at[kind, at.kp], piece(out, at.kp), w_recv.at[kind, at.kp])

    def place_in(kind, q):
        out = lw if kind == 0 else sw
        return remote(stage.at[kind, q], piece(out, q), w_send.at[kind, q], w_recv.at[kind, q], at.partner)

    def send_picked(kind):
        def pick(t):
            stage[kind, t] = z[src[t, kind]]

        def send(o):
            t = (at.kp + o + 1) % n
            place(kind, t, 0).start()

        loop(n, pick)
        loop(n - 1, send)

        @pl.when(at.home)
        def _():
            place_own(kind).start()

        @pl.when(at.away)
        def _():
            place(kind, at.kp, 0).start()

    relay(range(0, B_CHUNKS // 2))
    loop(n - 1, lambda o: spread_in(o).wait_recv())
    z_own.wait()
    send_picked(0)
    send_picked(1)
    relay(range(B_CHUNKS // 2, B_CHUNKS))
    forward(range(B_CHUNKS))

    for kind in (0, 1):

        @pl.when(at.home)
        def _():
            loop(n - 1, lambda o: place_in(kind, (at.kp + o + 1) % n).wait_recv())
            place_own(kind).wait()

        @pl.when(at.away)
        def _():
            loop(n, lambda q: place_in(kind, q).wait_recv())

    for k in range(B_CHUNKS):
        b_copy(0, ft, at.mate_slab, k, at.mate).wait_recv()
        b_copy(2, ft, at.diag_slab, k, at.mate).wait_recv()

    loop(n - 1, lambda o: spread(o).wait_send())
    for kind in (0, 1):
        loop(n - 1, lambda o: place(kind, (at.kp + o + 1) % n, 0).wait_send())

    @pl.when(at.home)
    def _():
        f_own.wait()
        p_own.wait()

    @pl.when(at.away)
    def _():
        for kind in (0, 1):
            place(kind, at.kp, 0).wait_send()
        for k in range(B_CHUNKS):
            b_copy(3, ft, at.y, k, at.partner).wait_send()
        p_swap.wait()

    for k in range(B_CHUNKS):
        for kind in range(3):
            b_copy(kind, ft, at.own_slab, k, at.mate).wait_send()


def spread_call(n, sources, lam, ft, pt):
    anywhere = pl.BlockSpec(memory_space=pl.ANY)
    rows = 2 * OO // n
    dma = pltpu.SemaphoreType.DMA
    return pl.pallas_call(
        functools.partial(spread_kernel, n),
        out_shape=(
            jax.ShapeDtypeStruct((OO, SLAB), BF),
            jax.ShapeDtypeStruct((OO, SLAB), BF),
            jax.ShapeDtypeStruct((4, SLAB, NAUX), BF),
            jax.ShapeDtypeStruct((SLAB, NAUX), BF),
        ),
        in_specs=[pl.BlockSpec(memory_space=pltpu.SMEM)] + [anywhere] * 3,
        out_specs=(anywhere,) * 4,
        scratch_shapes=[
            pltpu.VMEM((n, rows, SLAB // 2), BF),
            pltpu.VMEM((2, n, rows, SLAB // 2), BF),
            dma((n,)),
            dma((n,)),
            dma((2, n)),
            dma((2, n)),
            dma((4, B_CHUNKS)),
            dma((4, B_CHUNKS)),
            dma,
            dma,
            dma((2,)),
        ],
        compiler_params=pltpu.CompilerParams(collective_id=0, has_side_effects=True, vmem_limit_bytes=32 << 20),
        name="spread",
    )(sources, lam, ft, pt)


def widen_factor(raw, f):
    zero = jnp.zeros((PAD - V, NAUX), F32)

    def body(g):
        parts = [raw[s, rows_of(g, 2 * VS), :].astype(F32) for s in range(4)]
        out = []
        for h in range(2):
            out += [part[VS * h : VS * (h + 1)] for part in parts] + [zero]
        f[:, rows_of(g, 2 * PAD)] = jnp.concatenate(out, 0).astype(BF).T

    loop(V // 2, body)


FORM = 16


def form(left, f, w):
    def body(g):
        x = jnp.dot(left(), f[:, rows_of(g, FORM * PAD)], preferred_element_type=F32)
        for pair in range(VS // 2):
            two = x[2 * VS * pair : 2 * VS * (pair + 1)]
            for q in range(FORM // 2):
                lo = 2 * PAD * q
                even = jnp.concatenate([two[:VS, lo : lo + PAD], two[VS:, lo : lo + PAD]], 1)
                odd = jnp.concatenate([two[:VS, lo + PAD : lo + 2 * PAD], two[VS:, lo + PAD : lo + 2 * PAD]], 1)
                w[pair, pl.ds(pl.multiple_of(g * (FORM * VS) + 2 * VS * q, 2 * VS), 2 * VS), :] = jnp.concatenate(
                    [even, odd], 0
                ).astype(BF)

    loop(V // FORM, body)


def ladder(left, w, total, first):
    for pair in range(VS // 2):
        x = jnp.dot(left(), w[pair], preferred_element_type=F32)
        at = pl.ds(2 * PAD * pair, 2 * PAD)
        if first:
            total[:, at] = x
        else:
            total[:, at] += x


def work_kernel(
    lw, cyc, ptw, fall, g_in, out, raw, f, w, lall, gall, total, cycle, mine, theirs,
    l_send, l_recv, g_send, g_recv, o_send, o_recv, own_sem,
):
    at = Place()
    barrier = pltpu.get_barrier_semaphore()
    for device in (at.mate, at.cross, at.partner):
        pl.semaphore_signal(barrier, inc=1, device_id=device, device_id_type=MESH)
    pl.semaphore_wait(barrier, 3)

    def l_copy(kind, src, slab, device):
        return remote(src, lall.at[slab], l_send.at[kind], l_recv.at[kind], device)

    def g_copy(kind, src, slab, device):
        return remote(src, gall.at[slab], g_send.at[kind], g_recv.at[kind], device)

    l_copy(1, lw, at.own_slab, at.cross).start()
    l_copy(0, lw, at.own_slab, at.mate).start()
    l_own = pltpu.make_async_copy(lw, lall.at[at.own_slab], own_sem.at[0])
    f_own = pltpu.make_async_copy(fall, raw, own_sem.at[1])
    g_own = pltpu.make_async_copy(g_in, gall.at[at.own_slab], own_sem.at[2])
    f_own.start()
    l_own.start()

    @pl.when(at.home)
    def _():
        g_copy(1, g_in, at.own_slab, at.cross).start()
        g_copy(0, g_in, at.own_slab, at.mate).start()
        g_own.start()

    @pl.when(at.away)
    def _():
        g_copy(3, g_in, at.y, at.partner).start()

    def left(slab):
        return lambda: ptw[rows_of(slab, VS * VS), :]

    f_own.wait()
    widen_factor(raw, f)
    form(left(at.own_slab), f, w)
    l_own.wait()
    ladder(lambda: lall[at.own_slab], w, total, True)

    @pl.when(at.away)
    def _():
        g_copy(3, g_in, at.own_slab, at.partner).wait_recv()
        g_copy(1, gall.at[at.own_slab], at.own_slab, at.cross).start()
        g_copy(0, gall.at[at.own_slab], at.own_slab, at.mate).start()

    form(left(at.mate_slab), f, w)
    l_copy(0, lw, at.mate_slab, at.mate).wait_recv()
    ladder(lambda: lall[at.mate_slab], w, total, False)
    l_copy(1, lw, at.cross_slab, at.cross).wait_recv()
    l_copy(2, lall.at[at.cross_slab], at.cross_slab, at.mate).start()
    form(left(at.cross_slab), f, w)
    ladder(lambda: lall[at.cross_slab], w, total, False)
    form(left(at.diag_slab), f, w)
    l_copy(2, lw, at.diag_slab, at.mate).wait_recv()
    ladder(lambda: lall[at.diag_slab], w, total, False)

    g_copy(1, g_in, at.cross_slab, at.cross).wait_recv()
    g_copy(2, gall.at[at.cross_slab], at.cross_slab, at.mate).start()

    @pl.when(at.home)
    def _():
        g_own.wait()

    g_copy(0, g_in, at.mate_slab, at.mate).wait_recv()
    g_copy(2, g_in, at.diag_slab, at.mate).wait_recv()
    depth = VS * O

    def cycle_part(j):
        x = None
        for s in range(4):
            y = jnp.dot(cyc[:, depth * s : depth * (s + 1)], gall[s, :, rows_of(j, 4 * V)], preferred_element_type=F32)
            x = y if x is None else x + y
        cycle[:, rows_of(j, 4 * V)] = x

    loop(O // 4, cycle_part)

    def o_copy(m):
        cols = rows_of(m, 4 * V)
        return remote(mine.at[:, cols], theirs.at[:, cols], o_send.at[m], o_recv.at[m], at.partner)

    def finish(m):
        cols = []
        for r in range(4):
            rows = cycle[pl.ds(pl.multiple_of(m * (4 * O) + O * r, O), O), :]
            rows = jnp.concatenate([rows[:, V * j : V * (j + 1)] for j in range(O)], 0)
            lad = total[:, pl.ds(pl.multiple_of(m * (4 * PAD) + PAD * r, PAD), PAD)]
            cols.append(lad[:, :V] + rows)
        x = jnp.concatenate(cols, 1)

        @pl.when(at.home)
        def _():
            out[:, rows_of(m, 4 * V)] = x

        @pl.when(at.away)
        def _():
            mine[:, rows_of(m, 4 * V)] = x.astype(BF)
            o_copy(m).start()

    loop(VS // 4, finish)

    @pl.when(at.away)
    def _():
        def take(m):
            o_copy(m).wait_recv()
            out[:, rows_of(m, 4 * V)] = theirs[:, rows_of(m, 4 * V)].astype(F32)

        loop(VS // 4, take)
        loop(VS // 4, lambda m: o_copy(m).wait_send())
        g_copy(3, g_in, at.y, at.partner).wait_send()

    for kind in range(3):
        l_copy(kind, lw, at.own_slab, at.mate).wait_send()
        g_copy(kind, g_in, at.own_slab, at.mate).wait_send()


def work_call(lw, cyc, ptw, fall, g_in):
    anywhere = pl.BlockSpec(memory_space=pl.ANY)
    vmem = pl.BlockSpec(memory_space=pltpu.VMEM)
    dma = pltpu.SemaphoreType.DMA
    return pl.pallas_call(
        work_kernel,
        out_shape=jax.ShapeDtypeStruct((OO, SLAB), F32),
        in_specs=[anywhere, vmem, vmem, anywhere, anywhere],
        out_specs=vmem,
        scratch_shapes=[
            pltpu.VMEM((4, SLAB, NAUX), BF),
            pltpu.VMEM((NAUX, V * PAD), BF),
            pltpu.VMEM((VS // 2, SLAB, 2 * PAD), BF),
            pltpu.VMEM((4, OO, SLAB), BF),
            pltpu.VMEM((4, VS * O, O * V), BF),
            pltpu.VMEM((OO, VS * PAD), F32),
            pltpu.VMEM((VS * O, O * V), F32),
            pltpu.VMEM((OO, SLAB), BF),
            pltpu.VMEM((OO, SLAB), BF),
            dma((3,)),
            dma((3,)),
            dma((4,)),
            dma((4,)),
            dma((VS // 4,)),
            dma((VS // 4,)),
            dma((3,)),
        ],
        compiler_params=pltpu.CompilerParams(collective_id=1, has_side_effects=True, vmem_limit_bytes=63 << 20),
        name="work",
    )(lw, cyc, ptw, fall, g_in)


def local(n, lam, chol, cycle_int, sources):
    factor = chol[0].reshape(NAUX, VS, V)
    ft = jnp.transpose(factor, (2, 1, 0)).reshape(SLAB, NAUX)
    pt = jnp.transpose(factor.reshape(NAUX, VS, 4, VS), (2, 1, 3, 0)).reshape(SLAB, NAUX)
    lw, sw, fall, ptw = spread_call(n, sources, lam[0], ft, pt)
    lw = jnp.transpose(lw.reshape(O, O, VS, V), (1, 0, 3, 2)).reshape(OO, SLAB)
    cyc = jnp.transpose(sw.reshape(O, O, VS, V), (2, 0, 3, 1)).reshape(VS * O, V * O)
    out = work_call(lw, cyc, ptw, fall, cycle_int[0])
    out = jnp.transpose(out.reshape(O, O, SLAB), (1, 0, 2)).reshape(OO, SLAB)
    return out[None]


def solution(mesh):
    placed = (P("kpair", None, "vir"), P("kpair", None, "vir"), P("kpair", "vir", None), P())
    return jax.shard_map(
        functools.partial(local, mesh.shape["kpair"]),
        mesh=mesh,
        in_specs=placed,
        out_specs=P("kpair", None, "vir"),
        check_vma=False,
    )
```

```python
import functools

import jax
import jax.numpy as jnp
from jax import lax
from jax.experimental import pallas as pl
from jax.experimental.pallas import tpu as pltpu
from jax.sharding import PartitionSpec as P

O = 16
V = 96
VS = 24
NAUX = 384
OO = O * O
SLAB = VS * V
PAD = 128
BF = jnp.bfloat16
F32 = jnp.float32
MESH = pl.DeviceIdType.MESH
B_CHUNKS = 4


class Place:
    def __init__(self):
        kp = lax.axis_index("kpair")
        y = lax.axis_index("vir")
        core = kp % 2
        half = y // 2
        guest = (core + half) % 2
        other = y + 1 - 2 * (y % 2)
        swap = kp + 1 - 2 * core
        self.kp, self.y, self.half, self.guest = kp, y, half, guest
        self.home = guest == 0
        self.away = guest == 1
        self.mate = (swap, y)
        self.cross = (kp, other)
        self.partner = (swap, 3 - y)
        self.own_slab = y + guest * (3 - 2 * y)
        self.mate_slab = y + (1 - guest) * (3 - 2 * y)
        self.cross_slab = other + guest * (3 - 2 * other)
        self.diag_slab = other + (1 - guest) * (3 - 2 * other)


def remote(src, dst, send, recv, device):
    return pltpu.make_async_remote_copy(
        src_ref=src, dst_ref=dst, send_sem=send, recv_sem=recv, device_id=device, device_id_type=MESH
    )


def loop(count, body):
    def step(i, carry):
        body(i)
        return carry

    lax.fori_loop(0, count, step, 0)


def rows_of(index, size):
    return pl.ds(pl.multiple_of(index * size, size), size)


def spread_kernel(
    n, src, lam, ft, pt, lw, sw, fall, ptw, z, stage, z_send, z_recv, w_send, w_recv, b_send, b_recv, p_send, p_recv, own_sem
):
    at = Place()
    rows = 2 * OO // n
    lanes = SLAB // 2

    def piece(ref, q):
        return ref.at[rows_of(q // 2, rows), pl.ds(pl.multiple_of((q % 2) * lanes, 128), lanes)]

    barrier = pltpu.get_barrier_semaphore()

    def greet(o):
        pl.semaphore_signal(barrier, inc=1, device_id=((at.kp + o) % n, 3 - at.y), device_id_type=MESH)

    def greet_plane(o):
        pl.semaphore_signal(barrier, inc=1, device_id=((at.kp + o + 1) % n, at.y), device_id_type=MESH)

    pl.semaphore_signal(barrier, inc=1, device_id=at.cross, device_id_type=MESH)
    loop(n, greet)
    loop(n - 1, greet_plane)
    pl.semaphore_wait(barrier, 2 * n)

    def spread(o):
        q = (at.kp + o + 1) % n
        return remote(piece(lam, q), z.at[at.kp], z_send.at[q], z_recv.at[at.kp], (q, at.y))

    def spread_in(o):
        q = (at.kp + o + 1) % n
        return remote(piece(lam, at.kp), z.at[q], z_send.at[q], z_recv.at[q], (q, at.y))

    z_own = pltpu.make_async_copy(piece(lam, at.kp), z.at[at.kp], z_recv.at[at.kp])
    loop(n - 1, lambda o: spread(o).start())
    z_own.start()

    step = SLAB // B_CHUNKS

    def chunk(ref, k):
        return ref.at[pl.ds(k * step, step)]

    def b_copy(kind, src_ref, slab, k, device):
        return remote(chunk(src_ref, k), chunk(fall.at[slab], k), b_send.at[kind, k], b_recv.at[kind, k], device)

    f_own = pltpu.make_async_copy(ft, fall.at[at.own_slab], own_sem.at[0])
    p_own = pltpu.make_async_copy(pt, ptw, own_sem.at[1])
    p_swap = remote(pt, ptw, p_send, p_recv, at.partner)

    @pl.when(at.home)
    def _():
        for k in range(B_CHUNKS):
            b_copy(1, ft, at.own_slab, k, at.cross).start()
            b_copy(0, ft, at.own_slab, k, at.mate).start()
        f_own.start()
        p_own.start()

    @pl.when(at.away)
    def _():
        for k in range(B_CHUNKS):
            b_copy(3, ft, at.y, k, at.partner).start()
        p_swap.start()

    def relay(ks):
        @pl.when(at.away)
        def _():
            for k in ks:
                b_copy(3, ft, at.own_slab, k, at.partner).wait_recv()
                b_copy(1, fall.at[at.own_slab], at.own_slab, k, at.cross).start()
                b_copy(0, fall.at[at.own_slab], at.own_slab, k, at.mate).start()

    def forward(ks):
        for k in ks:
            b_copy(1, ft, at.cross_slab, k, at.cross).wait_recv()
            b_copy(2, fall.at[at.cross_slab], at.cross_slab, k, at.mate).start()

    def place(kind, t, q):
        e = t % 2
        moved = (e + at.half) % 2
        device = (t + moved * (1 - 2 * e), at.y + moved * (3 - 2 * at.y))
        out = lw if kind == 0 else sw
        return remote(stage.at[kind, t], piece(out, at.kp), w_send.at[kind, t], w_recv.at[kind, at.kp], device)

    def place_own(kind):
        out = lw if kind == 0 else sw
        return pltpu.make_async_copy(stage.at[kind, at.kp], piece(out, at.kp), w_recv.at[kind, at.kp])

    def place_in(kind, q):
        out = lw if kind == 0 else sw
        return remote(stage.at[kind, q], piece(out, q), w_send.at[kind, q], w_recv.at[kind, q], at.partner)

    def send_picked(kind):
        def pick(t):
            stage[kind, t] = z[src[t, kind]]

        def send(o):
            t = (at.kp + o + 1) % n
            place(kind, t, 0).start()

        loop(n, pick)
        loop(n - 1, send)

        @pl.when(at.home)
        def _():
            place_own(kind).start()

        @pl.when(at.away)
        def _():
            place(kind, at.kp, 0).start()

    relay(range(0, B_CHUNKS // 2))
    loop(n - 1, lambda o: spread_in(o).wait_recv())
    z_own.wait()
    send_picked(0)
    send_picked(1)
    relay(range(B_CHUNKS // 2, B_CHUNKS))
    forward(range(B_CHUNKS))

    for kind in (0, 1):

        @pl.when(at.home)
        def _():
            loop(n - 1, lambda o: place_in(kind, (at.kp + o + 1) % n).wait_recv())
            place_own(kind).wait()

        @pl.when(at.away)
        def _():
            loop(n, lambda q: place_in(kind, q).wait_recv())

    for k in range(B_CHUNKS):
        b_copy(0, ft, at.mate_slab, k, at.mate).wait_recv()
        b_copy(2, ft, at.diag_slab, k, at.mate).wait_recv()

    loop(n - 1, lambda o: spread(o).wait_send())
    for kind in (0, 1):
        loop(n - 1, lambda o: place(kind, (at.kp + o + 1) % n, 0).wait_send())

    @pl.when(at.home)
    def _():
        f_own.wait()
        p_own.wait()

    @pl.when(at.away)
    def _():
        for kind in (0, 1):
            place(kind, at.kp, 0).wait_send()
        for k in range(B_CHUNKS):
            b_copy(3, ft, at.y, k, at.partner).wait_send()
        p_swap.wait()

    for k in range(B_CHUNKS):
        for kind in range(3):
            b_copy(kind, ft, at.own_slab, k, at.mate).wait_send()


def spread_call(n, sources, lam, ft, pt):
    anywhere = pl.BlockSpec(memory_space=pl.ANY)
    rows = 2 * OO // n
    dma = pltpu.SemaphoreType.DMA
    return pl.pallas_call(
        functools.partial(spread_kernel, n),
        out_shape=(
            jax.ShapeDtypeStruct((OO, SLAB), BF),
            jax.ShapeDtypeStruct((OO, SLAB), BF),
            jax.ShapeDtypeStruct((4, SLAB, NAUX), BF),
            jax.ShapeDtypeStruct((SLAB, NAUX), BF),
        ),
        in_specs=[pl.BlockSpec(memory_space=pltpu.SMEM)] + [anywhere] * 3,
        out_specs=(anywhere,) * 4,
        scratch_shapes=[
            pltpu.VMEM((n, rows, SLAB // 2), BF),
            pltpu.VMEM((2, n, rows, SLAB // 2), BF),
            dma((n,)),
            dma((n,)),
            dma((2, n)),
            dma((2, n)),
            dma((4, B_CHUNKS)),
            dma((4, B_CHUNKS)),
            dma,
            dma,
            dma((2,)),
        ],
        compiler_params=pltpu.CompilerParams(collective_id=0, has_side_effects=True, vmem_limit_bytes=32 << 20),
        name="spread",
    )(sources, lam, ft, pt)


def widen_factor(raw, f):
    zero = jnp.zeros((PAD - V, NAUX), F32)

    def body(g):
        parts = [raw(s, rows_of(g, 2 * VS)).astype(F32) for s in range(4)]
        out = []
        for h in range(2):
            out += [part[VS * h : VS * (h + 1)] for part in parts] + [zero]
        f[:, rows_of(g, 2 * PAD)] = jnp.concatenate(out, 0).astype(BF).T

    loop(V // 2, body)


def one_hot(size, outer, inner):
    row = lax.broadcasted_iota(jnp.int32, (size, size), 0)
    col = lax.broadcasted_iota(jnp.int32, (size, size), 1)
    x = lax.shift_right_logical(col, inner.bit_length() - 1)
    y = lax.bitwise_and(col, inner - 1)
    return jnp.where(row == y * outer + x, 1.0, 0.0).astype(BF)


def flip_pairs(lw, turned, flat):
    wide = 4 * V
    for g in range(SLAB // wide):
        x = lw[:, wide * g : wide * (g + 1)].astype(F32).T
        for h in range(2):
            turned[h, wide * g : wide * (g + 1), :] = x[:, PAD * h : PAD * (h + 1)]
    for g in range(V // O):
        x = [
            jnp.concatenate([turned[h, pl.ds(O * g + d, VS, stride=V), :] for d in range(O)], 0) for h in range(2)
        ]
        flat[:, wide * g : wide * (g + 1)] = jnp.concatenate(x, 1).astype(BF).T


def cycle_left(sw, swap, cyc):
    def body(g):
        x = jnp.dot(swap, sw[:, rows_of(g, 4 * V)], preferred_element_type=F32)
        for r in range(4):
            for m in range(4):
                part = [x[O * k : O * (k + 1), V * r : V * (r + 1)] for k in range(4 * m, 4 * m + 4)]
                cyc[pl.ds(pl.multiple_of(g * (4 * O) + O * r, O), O), 4 * V * m : 4 * V * (m + 1)] = jnp.concatenate(
                    part, 1
                ).astype(BF)

    loop(VS // 4, body)


def cycle_right(gall, swap, cols, right):
    parts = [jnp.dot(swap, gall[s, :, cols], preferred_element_type=F32) for s in range(4)]
    for k in range(O):
        right[V * k : V * (k + 1), :] = jnp.concatenate([part[VS * k : VS * (k + 1)] for part in parts], 0).astype(BF)


FORM = 16


def form(left, f, w):
    def body(g):
        x = jnp.dot(left(), f[:, rows_of(g, FORM * PAD)], preferred_element_type=F32)
        for pair in range(VS // 2):
            two = x[2 * VS * pair : 2 * VS * (pair + 1)]
            for q in range(FORM // 2):
                lo = 2 * PAD * q
                even = jnp.concatenate([two[:VS, lo : lo + PAD], two[VS:, lo : lo + PAD]], 1)
                odd = jnp.concatenate([two[:VS, lo + PAD : lo + 2 * PAD], two[VS:, lo + PAD : lo + 2 * PAD]], 1)
                w[pair, pl.ds(pl.multiple_of(g * (FORM * VS) + 2 * VS * q, 2 * VS), 2 * VS), :] = jnp.concatenate(
                    [even, odd], 0
                ).astype(BF)

    loop(V // FORM, body)


def ladder(left, w, total, first):
    for pair in range(VS // 2):
        x = jnp.dot(left(), w[pair], preferred_element_type=F32)
        at = pl.ds(2 * PAD * pair, 2 * PAD)
        if first:
            total[:, at] = x
        else:
            total[:, at] += x


def work_kernel(
    lw, sw, ptw, fall, g_in, out, f, w, lall, gall, total, turned, cyc, right, cycle, tall, mine, theirs,
    l_send, l_recv, g_send, g_recv, o_send, o_recv, own_sem, f_sem,
):
    at = Place()
    barrier = pltpu.get_barrier_semaphore()
    for device in (at.mate, at.cross, at.partner):
        pl.semaphore_signal(barrier, inc=1, device_id=device, device_id_type=MESH)
    pl.semaphore_wait(barrier, 3)

    def l_copy(kind, slab, device):
        return remote(lall.at[slab], lall.at[slab], l_send.at[kind], l_recv.at[kind], device)

    def g_copy(kind, src, slab, device):
        return remote(src, gall.at[slab], g_send.at[kind], g_recv.at[kind], device)

    g_own = pltpu.make_async_copy(g_in, gall.at[at.own_slab], own_sem)
    wide = 2 * PAD
    raw = []
    for s in range(4):
        raw.append(pltpu.make_async_copy(fall.at[s, :, pl.ds(0, wide)], w.at[2 * s], f_sem.at[s, 0]))
        raw.append(
            pltpu.make_async_copy(
                fall.at[s, :, pl.ds(wide, NAUX - wide)], w.at[2 * s + 1, :, pl.ds(0, NAUX - wide)], f_sem.at[s, 1]
            )
        )
    for copy in raw:
        copy.start()

    flip_pairs(lw, turned, lall.at[at.own_slab])
    l_copy(1, at.own_slab, at.cross).start()
    l_copy(0, at.own_slab, at.mate).start()

    @pl.when(at.home)
    def _():
        g_copy(1, g_in, at.own_slab, at.cross).start()
        g_copy(0, g_in, at.own_slab, at.mate).start()
        g_own.start()

    @pl.when(at.away)
    def _():
        g_copy(3, g_in, at.y, at.partner).start()

    def left(slab):
        return lambda: ptw[rows_of(slab, VS * VS), :]

    for copy in raw:
        copy.wait()
    widen_factor(
        lambda s, rows: jnp.concatenate([w[2 * s, rows, :], w[2 * s + 1, rows, : NAUX - wide]], 1), f
    )
    form(left(at.own_slab), f, w)
    ladder(lambda: lall[at.own_slab], w, total, True)

    @pl.when(at.away)
    def _():
        g_copy(3, g_in, at.own_slab, at.partner).wait_recv()
        g_copy(1, gall.at[at.own_slab], at.own_slab, at.cross).start()
        g_copy(0, gall.at[at.own_slab], at.own_slab, at.mate).start()

    form(left(at.mate_slab), f, w)
    l_copy(0, at.mate_slab, at.mate).wait_recv()
    ladder(lambda: lall[at.mate_slab], w, total, False)
    l_copy(1, at.cross_slab, at.cross).wait_recv()
    l_copy(2, at.cross_slab, at.mate).start()
    form(left(at.cross_slab), f, w)
    ladder(lambda: lall[at.cross_slab], w, total, False)
    cycle_left(sw, one_hot(OO, O, O), cyc)
    form(left(at.diag_slab), f, w)
    l_copy(2, at.diag_slab, at.mate).wait_recv()
    ladder(lambda: lall[at.diag_slab], w, total, False)

    g_copy(1, g_in, at.cross_slab, at.cross).wait_recv()
    g_copy(2, gall.at[at.cross_slab], at.cross_slab, at.mate).start()

    @pl.when(at.home)
    def _():
        g_own.wait()

    g_copy(0, g_in, at.mate_slab, at.mate).wait_recv()
    g_copy(2, g_in, at.diag_slab, at.mate).wait_recv()
    swap = one_hot(VS * O, VS, O)

    def cycle_part(j):
        cols = rows_of(j, 4 * V)
        cycle_right(gall, swap, cols, right)
        cycle[:, cols] = jnp.dot(cyc[...], right[...], preferred_element_type=F32)

    loop(O // 4, cycle_part)

    def o_copy(m):
        cols = rows_of(m, 4 * V)
        return remote(mine.at[:, cols], theirs.at[:, cols], o_send.at[m], o_recv.at[m], at.partner)

    def finish(m):
        cols = []
        for r in range(4):
            rows = cycle[pl.ds(pl.multiple_of(m * (4 * O) + O * r, O), O), :]
            for j in range(O):
                tall[r, pl.ds(j, O, stride=O), :V] = rows[:, V * j : V * (j + 1)]
            lad = total[:, pl.ds(pl.multiple_of(m * (4 * PAD) + PAD * r, PAD), PAD)]
            cols.append(lad[:, :V] + tall[r, :, :V])
        x = jnp.concatenate(cols, 1)

        @pl.when(at.home)
        def _():
            out[:, rows_of(m, 4 * V)] = x

        @pl.when(at.away)
        def _():
            mine[:, rows_of(m, 4 * V)] = x.astype(BF)
            o_copy(m).start()

    loop(VS // 4, finish)

    @pl.when(at.away)
    def _():
        def take(m):
            o_copy(m).wait_recv()
            out[:, rows_of(m, 4 * V)] = theirs[:, rows_of(m, 4 * V)].astype(F32)

        loop(VS // 4, take)
        loop(VS // 4, lambda m: o_copy(m).wait_send())
        g_copy(3, g_in, at.y, at.partner).wait_send()

    for kind in range(3):
        l_copy(kind, at.own_slab, at.mate).wait_send()
        g_copy(kind, g_in, at.own_slab, at.mate).wait_send()


def work_call(lw, sw, ptw, fall, g_in):
    anywhere = pl.BlockSpec(memory_space=pl.ANY)
    vmem = pl.BlockSpec(memory_space=pltpu.VMEM)
    dma = pltpu.SemaphoreType.DMA
    return pl.pallas_call(
        work_kernel,
        out_shape=jax.ShapeDtypeStruct((OO, SLAB), F32),
        in_specs=[vmem, vmem, vmem, anywhere, anywhere],
        out_specs=vmem,
        scratch_shapes=[
            pltpu.VMEM((NAUX, V * PAD), BF),
            pltpu.VMEM((VS // 2, SLAB, 2 * PAD), BF),
            pltpu.VMEM((4, OO, SLAB), BF),
            pltpu.VMEM((4, VS * O, O * V), BF),
            pltpu.VMEM((OO, VS * PAD), F32),
            pltpu.VMEM((2, SLAB, PAD), F32),
            pltpu.VMEM((VS * O, O * V), BF),
            pltpu.VMEM((O * V, 4 * V), BF),
            pltpu.VMEM((VS * O, O * V), F32),
            pltpu.VMEM((4, OO, PAD), F32),
            pltpu.VMEM((OO, SLAB), BF),
            pltpu.VMEM((OO, SLAB), BF),
            dma((3,)),
            dma((3,)),
            dma((4,)),
            dma((4,)),
            dma((VS // 4,)),
            dma((VS // 4,)),
            dma,
            dma((4, 2)),
        ],
        compiler_params=pltpu.CompilerParams(collective_id=1, has_side_effects=True, vmem_limit_bytes=63 << 20),
        name="work",
    )(lw, sw, ptw, fall, g_in)


def local(n, lam, chol, cycle_int, sources):
    factor = chol[0].reshape(NAUX, VS, V)
    ft = jnp.transpose(factor, (2, 1, 0)).reshape(SLAB, NAUX)
    pt = jnp.transpose(factor.reshape(NAUX, VS, 4, VS), (2, 1, 3, 0)).reshape(SLAB, NAUX)
    lw, sw, fall, ptw = spread_call(n, sources, lam[0], ft, pt)
    out = work_call(lw, sw, ptw, fall, cycle_int[0])
    return out[None]


def solution(mesh):
    placed = (P("kpair", None, "vir"), P("kpair", None, "vir"), P("kpair", "vir", None), P())
    return jax.shard_map(
        functools.partial(local, mesh.shape["kpair"]),
        mesh=mesh,
        in_specs=placed,
        out_specs=P("kpair", None, "vir"),
        check_vma=False,
    )
```

```python
import functools

import jax
import jax.numpy as jnp
from jax import lax
from jax.experimental import pallas as pl
from jax.experimental.pallas import tpu as pltpu
from jax.sharding import PartitionSpec as P

O = 16
V = 96
VS = 24
NAUX = 384
OO = O * O
SLAB = VS * V
PAD = 128
BF = jnp.bfloat16
F32 = jnp.float32
MESH = pl.DeviceIdType.MESH
D_CHUNKS = 3
DC = V // D_CHUNKS
CROWS = DC * VS


class Place:
    def __init__(self):
        kp = lax.axis_index("kpair")
        y = lax.axis_index("vir")
        core = kp % 2
        half = y // 2
        guest = (core + half) % 2
        other = y + 1 - 2 * (y % 2)
        swap = kp + 1 - 2 * core
        self.kp, self.y, self.half, self.guest = kp, y, half, guest
        self.home = guest == 0
        self.away = guest == 1
        self.mate = (swap, y)
        self.cross = (kp, other)
        self.partner = (swap, 3 - y)
        self.own_slab = y + guest * (3 - 2 * y)
        self.mate_slab = y + (1 - guest) * (3 - 2 * y)
        self.cross_slab = other + guest * (3 - 2 * other)
        self.diag_slab = other + (1 - guest) * (3 - 2 * other)


def remote(src, dst, send, recv, device):
    return pltpu.make_async_remote_copy(
        src_ref=src, dst_ref=dst, send_sem=send, recv_sem=recv, device_id=device, device_id_type=MESH
    )


def loop(count, body):
    def step(i, carry):
        body(i)
        return carry

    lax.fori_loop(0, count, step, 0)


def rows_of(index, size):
    return pl.ds(pl.multiple_of(index * size, size), size)


def widen_factor(raw, f, k):
    zero = jnp.zeros((PAD - V, NAUX), F32)

    def body(g):
        parts = [
            raw[pl.ds(pl.multiple_of(g * (2 * VS) + CROWS * s, 2 * VS), 2 * VS), :].astype(F32) for s in range(4)
        ]
        out = []
        for h in range(2):
            out += [part[VS * h : VS * (h + 1)] for part in parts] + [zero]
        f[:, rows_of(g + k * (DC // 2), 2 * PAD)] = jnp.concatenate(out, 0).astype(BF).T

    loop(DC // 2, body)


FORM = 16


def form(left, f, k, w):
    def body(g):
        x = jnp.dot(left(), f[:, rows_of(g + k * (DC // FORM), FORM * PAD)], preferred_element_type=F32)
        for pair in range(VS // 2):
            two = x[2 * VS * pair : 2 * VS * (pair + 1)]
            for q in range(FORM // 2):
                lo = 2 * PAD * q
                even = jnp.concatenate([two[:VS, lo : lo + PAD], two[VS:, lo : lo + PAD]], 1)
                odd = jnp.concatenate([two[:VS, lo + PAD : lo + 2 * PAD], two[VS:, lo + PAD : lo + 2 * PAD]], 1)
                w[pair, pl.ds(pl.multiple_of(g * (FORM * VS) + 2 * VS * q, 2 * VS), 2 * VS), :] = jnp.concatenate(
                    [even, odd], 0
                ).astype(BF)

    loop(DC // FORM, body)


def ladder(left, w, total):
    for pair in range(VS // 2):
        total[:, 2 * PAD * pair : 2 * PAD * (pair + 1)] += jnp.dot(left(), w[pair], preferred_element_type=F32)


def one_hot(size, outer, inner):
    row = lax.broadcasted_iota(jnp.int32, (size, size), 0)
    col = lax.broadcasted_iota(jnp.int32, (size, size), 1)
    x = lax.shift_right_logical(col, inner.bit_length() - 1)
    y = lax.bitwise_and(col, inner - 1)
    return jnp.where(row == y * outer + x, 1.0, 0.0).astype(BF)


def first_factor(raw, plane, left):
    for h in range(NAUX // PAD):
        lanes = slice(PAD * h, PAD * (h + 1))
        plane[...] = raw[:SLAB, lanes].astype(F32)

        def body(s):
            for a in range(0, VS, 2):
                two = [plane[pl.ds(VS * VS * s + a + e, VS, stride=VS), :] for e in range(2)]
                left[pl.ds(pl.multiple_of(s * (VS * VS) + VS * a, 2 * VS), 2 * VS), lanes] = jnp.concatenate(
                    two, 0
                ).astype(BF)

        loop(4, body)


def flip_pairs(lw, plane, flat):
    wide = 4 * V
    for h in range(OO // PAD):
        rows = slice(PAD * h, PAD * (h + 1))
        for g in range(SLAB // wide):
            plane[wide * g : wide * (g + 1), :] = lw[rows, wide * g : wide * (g + 1)].astype(F32).T
        for g in range(V // O):
            x = jnp.concatenate([plane[pl.ds(O * g + d, VS, stride=V), :] for d in range(O)], 0)
            flat[rows, wide * g : wide * (g + 1)] = x.astype(BF).T


def cycle_left(sw, swap, cyc):
    def body(g):
        x = jnp.dot(swap, sw[:, rows_of(g, 4 * V)], preferred_element_type=F32)
        for r in range(4):
            for m in range(4):
                part = [x[O * k : O * (k + 1), V * r : V * (r + 1)] for k in range(4 * m, 4 * m + 4)]
                cyc[pl.ds(pl.multiple_of(g * (4 * O) + O * r, O), O), 4 * V * m : 4 * V * (m + 1)] = jnp.concatenate(
                    part, 1
                ).astype(BF)

    loop(VS // 4, body)


def cycle_right(part, swap, right):
    slabs = [jnp.dot(swap, part[s], preferred_element_type=F32) for s in range(4)]
    for k in range(O):
        right[V * k : V * (k + 1), :] = jnp.concatenate([x[VS * k : VS * (k + 1)] for x in slabs], 0).astype(BF)


G_CHUNKS = 4
GC = O * V // G_CHUNKS


def kernel(
    n, src, lam, ft, g_in, out, fall, gall, z, stage, lw, sw, raw, f, w, lall, total, plane, left, cyc, part, right,
    cycle, tall, mine, theirs, z_send, z_recv, w_send, w_recv, b_send, b_recv, l_send, l_recv, g_send, g_recv, o_send,
    o_recv, raw_sem, part_sem,
):
    at = Place()
    rows = 2 * OO // n
    lanes = SLAB // 2

    def piece(ref, q):
        return ref.at[rows_of(q // 2, rows), pl.ds(pl.multiple_of((q % 2) * lanes, 128), lanes)]

    barrier = pltpu.get_barrier_semaphore()

    def greet(o):
        pl.semaphore_signal(barrier, inc=1, device_id=((at.kp + o) % n, 3 - at.y), device_id_type=MESH)

    def greet_plane(o):
        pl.semaphore_signal(barrier, inc=1, device_id=((at.kp + o + 1) % n, at.y), device_id_type=MESH)

    pl.semaphore_signal(barrier, inc=1, device_id=at.cross, device_id_type=MESH)
    loop(n, greet)
    loop(n - 1, greet_plane)
    pl.semaphore_wait(barrier, 2 * n)

    def spread(o):
        q = (at.kp + o + 1) % n
        return remote(piece(lam, q), z.at[at.kp], z_send.at[q], z_recv.at[at.kp], (q, at.y))

    def spread_in(o):
        q = (at.kp + o + 1) % n
        return remote(piece(lam, at.kp), z.at[q], z_send.at[q], z_recv.at[q], (q, at.y))

    z_own = pltpu.make_async_copy(piece(lam, at.kp), z.at[at.kp], z_recv.at[at.kp])

    def place(kind, t):
        e = t % 2
        moved = (e + at.half) % 2
        device = (t + moved * (1 - 2 * e), at.y + moved * (3 - 2 * at.y))
        to = (lw, sw)[kind]
        return remote(stage.at[kind, t], piece(to, at.kp), w_send.at[kind, t], w_recv.at[kind, at.kp], device)

    def place_own(kind):
        return pltpu.make_async_copy(stage.at[kind, at.kp], piece((lw, sw)[kind], at.kp), w_recv.at[kind, at.kp])

    def place_in(kind, q):
        to = (lw, sw)[kind]
        return remote(stage.at[kind, q], piece(to, q), w_send.at[kind, q], w_recv.at[kind, q], at.partner)

    def send_picked(kind):
        def pick(t):
            stage[kind, t] = z[src[t, kind]]

        loop(n, pick)
        loop(n - 1, lambda o: place(kind, (at.kp + o + 1) % n).start())

        @pl.when(at.home)
        def _():
            place_own(kind).start()

        @pl.when(at.away)
        def _():
            place(kind, at.kp).start()

    def take_picked(kind):
        @pl.when(at.home)
        def _():
            loop(n - 1, lambda o: place_in(kind, (at.kp + o + 1) % n).wait_recv())
            place_own(kind).wait()

        @pl.when(at.away)
        def _():
            loop(n, lambda q: place_in(kind, q).wait_recv())

    def b_copy(kind, src_ref, slab, k, device):
        cut = pl.ds(CROWS * k, CROWS)
        return remote(src_ref.at[cut], fall.at[slab, cut], b_send.at[kind, k], b_recv.at[kind, k], device)

    def l_copy(kind, slab, device):
        return remote(lall.at[slab], lall.at[slab], l_send.at[kind], l_recv.at[kind], device)

    def g_copy(kind, src_ref, slab, j, device):
        cut = pl.ds(GC * j, GC)
        return remote(src_ref.at[:, cut], gall.at[slab, :, cut], g_send.at[kind, j], g_recv.at[kind, j], device)

    def fetch(mine, theirs, to, sem):
        @pl.when(at.home)
        def _():
            pltpu.make_async_copy(mine, to, sem).start()

        @pl.when(at.away)
        def _():
            pltpu.make_async_copy(theirs, to, sem).start()

    loop(n - 1, lambda o: spread(o).start())
    z_own.start()

    @pl.when(at.home)
    def _():
        for k in range(D_CHUNKS):
            b_copy(1, ft, at.own_slab, k, at.cross).start()
            b_copy(0, ft, at.own_slab, k, at.mate).start()

    @pl.when(at.away)
    def _():
        for k in range(D_CHUNKS):
            b_copy(3, ft, at.y, k, at.partner).start()
        for k in range(D_CHUNKS):
            b_copy(3, ft, at.own_slab, k, at.partner).wait_recv()
            b_copy(1, fall.at[at.own_slab], at.own_slab, k, at.cross).start()
            b_copy(0, fall.at[at.own_slab], at.own_slab, k, at.mate).start()
        for j in range(G_CHUNKS):
            g_copy(3, g_in, at.y, j, at.partner).start()

    def forward(k):
        b_copy(1, ft, at.cross_slab, k, at.cross).wait_recv()
        b_copy(2, fall.at[at.cross_slab], at.cross_slab, k, at.mate).start()

    def send_g(j):
        @pl.when(at.home)
        def _():
            g_copy(1, g_in, at.own_slab, j, at.cross).start()
            g_copy(0, g_in, at.own_slab, j, at.mate).start()

        @pl.when(at.away)
        def _():
            g_copy(3, g_in, at.own_slab, j, at.partner).wait_recv()
            g_copy(1, gall.at[at.own_slab], at.own_slab, j, at.cross).start()
            g_copy(0, gall.at[at.own_slab], at.own_slab, j, at.mate).start()

    def forward_g(j):
        g_copy(1, g_in, at.cross_slab, j, at.cross).wait_recv()
        g_copy(2, gall.at[at.cross_slab], at.cross_slab, j, at.mate).start()

    total[...] = jnp.zeros_like(total)

    fetch(ft, fall.at[at.own_slab], raw.at[pl.ds(0, SLAB)], raw_sem.at[0])
    pltpu.make_async_copy(ft, raw.at[pl.ds(0, SLAB)], raw_sem.at[0]).wait()
    first_factor(raw, plane, left)
    forward(0)
    loop(n - 1, lambda o: spread_in(o).wait_recv())
    z_own.wait()
    send_picked(0)

    def prepare(k):
        b_copy(0, ft, at.mate_slab, k, at.mate).wait_recv()
        b_copy(2, ft, at.diag_slab, k, at.mate).wait_recv()
        cut = pl.ds(CROWS * k, CROWS)
        slabs = (at.own_slab, at.mate_slab, at.cross_slab, at.diag_slab)
        copies = [
            pltpu.make_async_copy(fall.at[slab, cut], raw.at[rows_of(slab, CROWS)], raw_sem.at[i])
            for i, slab in enumerate(slabs)
        ]
        fetch(ft.at[cut], fall.at[at.own_slab, cut], raw.at[rows_of(at.own_slab, CROWS)], raw_sem.at[0])
        for copy in copies[1:]:
            copy.start()
        for copy in copies:
            copy.wait()
        widen_factor(raw, f, k)

    def pick_slab(far, e):
        near = (at.own_slab, at.mate_slab) if not far else (at.cross_slab, at.diag_slab)
        return near[0] + e * (near[1] - near[0])

    def form_pair(far, k, slot):
        def body(e):
            slab = pick_slab(far, e)
            form(lambda: left[rows_of(slab, VS * VS), :], f, k, w.at[slot + e])

        loop(2, body)

    def ladder_pairs(far, k, slot, count):
        def body(i):
            slab = pick_slab(far, i % 2)
            cut = rows_of(k + i // 2, CROWS)
            ladder(lambda: lall[slab, :, cut], w.at[slot + i], total)

        loop(2 * count, body)

    forward(1)
    prepare(0)
    form_pair(False, 0, 0)
    prepare(1)
    form_pair(False, 1, 2)
    forward(2)
    send_g(0)
    take_picked(0)
    flip_pairs(lw, plane, lall.at[at.own_slab])
    l_copy(1, at.own_slab, at.cross).start()
    l_copy(0, at.own_slab, at.mate).start()
    send_picked(1)
    l_copy(0, at.mate_slab, at.mate).wait_recv()
    ladder_pairs(False, 0, 0, 2)
    prepare(2)
    form_pair(False, 2, 0)
    ladder_pairs(False, 2, 0, 1)
    form_pair(True, 0, 0)
    for j in range(1, G_CHUNKS):
        send_g(j)
    form_pair(True, 1, 2)
    l_copy(1, at.cross_slab, at.cross).wait_recv()
    l_copy(2, at.cross_slab, at.mate).start()
    take_picked(1)
    cycle_left(sw, one_hot(OO, O, O), cyc)
    l_copy(2, at.diag_slab, at.mate).wait_recv()
    ladder_pairs(True, 0, 0, 2)
    forward_g(0)
    form_pair(True, 2, 0)
    ladder_pairs(True, 2, 0, 1)
    for j in range(1, G_CHUNKS):
        forward_g(j)

    swap = one_hot(VS * O, VS, O)
    for j in range(G_CHUNKS):
        g_copy(0, g_in, at.mate_slab, j, at.mate).wait_recv()
        g_copy(2, g_in, at.diag_slab, j, at.mate).wait_recv()

    def cycle_part(j):
        cols = rows_of(j, GC)
        slabs = (at.own_slab, at.mate_slab, at.cross_slab, at.diag_slab)
        copies = [
            pltpu.make_async_copy(gall.at[slab, :, cols], part.at[slab], part_sem.at[i])
            for i, slab in enumerate(slabs)
        ]
        fetch(g_in.at[:, cols], gall.at[at.own_slab, :, cols], part.at[at.own_slab], part_sem.at[0])
        for copy in copies[1:]:
            copy.start()
        for copy in copies:
            copy.wait()
        cycle_right(part, swap, right)
        cycle[:, cols] = jnp.dot(cyc[...], right[...], preferred_element_type=F32)

    loop(G_CHUNKS, cycle_part)

    def o_copy(m):
        cols = rows_of(m, 4 * V)
        return remote(mine.at[:, cols], theirs.at[:, cols], o_send.at[m], o_recv.at[m], at.partner)

    def finish(m):
        cols = []
        for r in range(4):
            some = cycle[pl.ds(pl.multiple_of(m * (4 * O) + O * r, O), O), :]
            for j in range(O):
                tall[r, pl.ds(j, O, stride=O), :V] = some[:, V * j : V * (j + 1)]
            lad = total[:, pl.ds(pl.multiple_of(m * (4 * PAD) + PAD * r, PAD), PAD)]
            cols.append(lad[:, :V] + tall[r, :, :V])
        x = jnp.concatenate(cols, 1)

        @pl.when(at.home)
        def _():
            out[:, rows_of(m, 4 * V)] = x

        @pl.when(at.away)
        def _():
            mine[:, rows_of(m, 4 * V)] = x.astype(BF)
            o_copy(m).start()

    loop(VS // 4, finish)

    @pl.when(at.away)
    def _():
        def take(m):
            o_copy(m).wait_recv()
            out[:, rows_of(m, 4 * V)] = theirs[:, rows_of(m, 4 * V)].astype(F32)

        loop(VS // 4, take)
        loop(VS // 4, lambda m: o_copy(m).wait_send())

    loop(n - 1, lambda o: spread(o).wait_send())
    for kind in range(2):
        loop(n - 1, lambda o: place(kind, (at.kp + o + 1) % n).wait_send())

    @pl.when(at.away)
    def _():
        for kind in range(2):
            place(kind, at.kp).wait_send()
        for k in range(D_CHUNKS):
            b_copy(3, ft, at.y, k, at.partner).wait_send()
        for j in range(G_CHUNKS):
            g_copy(3, g_in, at.y, j, at.partner).wait_send()

    for kind in range(3):
        l_copy(kind, at.own_slab, at.mate).wait_send()
        for k in range(D_CHUNKS):
            b_copy(kind, ft, at.own_slab, k, at.mate).wait_send()
        for j in range(G_CHUNKS):
            g_copy(kind, g_in, at.own_slab, j, at.mate).wait_send()


def call(n, sources, lam, ft, g_in):
    anywhere = pl.BlockSpec(memory_space=pl.ANY)
    dma = pltpu.SemaphoreType.DMA
    rows = 2 * OO // n
    out, _, _ = pl.pallas_call(
        functools.partial(kernel, n),
        out_shape=(
            jax.ShapeDtypeStruct((OO, SLAB), F32),
            jax.ShapeDtypeStruct((4, SLAB, NAUX), BF),
            jax.ShapeDtypeStruct((4, VS * O, O * V), BF),
        ),
        in_specs=[pl.BlockSpec(memory_space=pltpu.SMEM)] + [anywhere] * 3,
        out_specs=(pl.BlockSpec(memory_space=pltpu.VMEM), anywhere, anywhere),
        scratch_shapes=[
            pltpu.VMEM((n, rows, SLAB // 2), BF),
            pltpu.VMEM((2, n, rows, SLAB // 2), BF),
            pltpu.VMEM((OO, SLAB), BF),
            pltpu.VMEM((OO, SLAB), BF),
            pltpu.VMEM((4 * CROWS, NAUX), BF),
            pltpu.VMEM((NAUX, V * PAD), BF),
            pltpu.VMEM((4, VS // 2, CROWS, 2 * PAD), BF),
            pltpu.VMEM((4, OO, SLAB), BF),
            pltpu.VMEM((OO, VS * PAD), F32),
            pltpu.VMEM((SLAB, PAD), F32),
            pltpu.VMEM((SLAB, NAUX), BF),
            pltpu.VMEM((VS * O, O * V), BF),
            pltpu.VMEM((4, VS * O, GC), BF),
            pltpu.VMEM((O * V, GC), BF),
            pltpu.VMEM((VS * O, O * V), F32),
            pltpu.VMEM((4, OO, PAD), F32),
            pltpu.VMEM((OO, SLAB), BF),
            pltpu.VMEM((OO, SLAB), BF),
            dma((n,)),
            dma((n,)),
            dma((2, n)),
            dma((2, n)),
            dma((4, D_CHUNKS)),
            dma((4, D_CHUNKS)),
            dma((3,)),
            dma((3,)),
            dma((4, G_CHUNKS)),
            dma((4, G_CHUNKS)),
            dma((VS // 4,)),
            dma((VS // 4,)),
            dma((4,)),
            dma((4,)),
        ],
        compiler_params=pltpu.CompilerParams(collective_id=0, has_side_effects=True, vmem_limit_bytes=63 << 20),
        name="residual",
    )(sources, lam, ft, g_in)
    return out


def local(n, lam, chol, cycle_int, sources):
    ft = jnp.transpose(chol[0].reshape(NAUX, VS, V), (2, 1, 0)).reshape(SLAB, NAUX)
    return call(n, sources, lam[0], ft, cycle_int[0])[None]


def solution(mesh):
    placed = (P("kpair", None, "vir"), P("kpair", None, "vir"), P("kpair", "vir", None), P())
    return jax.shard_map(
        functools.partial(local, mesh.shape["kpair"]),
        mesh=mesh,
        in_specs=placed,
        out_specs=P("kpair", None, "vir"),
        check_vma=False,
    )
```

```python
import functools

import jax
import jax.numpy as jnp
from jax import lax
from jax.experimental import pallas as pl
from jax.experimental.pallas import tpu as pltpu
from jax.sharding import PartitionSpec as P

O = 16
V = 96
VS = 24
NAUX = 384
OO = O * O
SLAB = VS * V
PAD = 128
BF = jnp.bfloat16
F32 = jnp.float32
MESH = pl.DeviceIdType.MESH
D_CHUNKS = 3
DC = V // D_CHUNKS
CROWS = DC * VS


class Place:
    def __init__(self):
        kp = lax.axis_index("kpair")
        y = lax.axis_index("vir")
        core = kp % 2
        half = y // 2
        guest = (core + half) % 2
        other = y + 1 - 2 * (y % 2)
        swap = kp + 1 - 2 * core
        self.kp, self.y, self.half, self.guest = kp, y, half, guest
        self.home = guest == 0
        self.away = guest == 1
        self.mate = (swap, y)
        self.cross = (kp, other)
        self.partner = (swap, 3 - y)
        self.own_slab = y + guest * (3 - 2 * y)
        self.mate_slab = y + (1 - guest) * (3 - 2 * y)
        self.cross_slab = other + guest * (3 - 2 * other)
        self.diag_slab = other + (1 - guest) * (3 - 2 * other)


def remote(src, dst, send, recv, device):
    return pltpu.make_async_remote_copy(
        src_ref=src, dst_ref=dst, send_sem=send, recv_sem=recv, device_id=device, device_id_type=MESH
    )


def loop(count, body):
    def step(i, carry):
        body(i)
        return carry

    lax.fori_loop(0, count, step, 0)


def rows_of(index, size):
    return pl.ds(pl.multiple_of(index * size, size), size)


def merge_factor(raw, f, k):
    def body(g):
        parts = [
            raw[pl.ds(pl.multiple_of(g * (4 * VS) + CROWS * s, 2 * VS), 4 * VS), :].astype(F32) for s in range(4)
        ]
        out = [part[VS * h : VS * (h + 1)] for h in range(4) for part in parts]
        f[:, rows_of(g + k * (DC // 4), 4 * V)] = jnp.concatenate(out, 0).astype(BF).T

    loop(DC // 4, body)


PAIRS = 4


def form(left, f, k, w):
    lane = lax.broadcasted_iota(jnp.int32, (2 * VS, PAD), 1)

    def body(m):
        x = jnp.dot(left(m), f[:, rows_of(k, DC * V)], preferred_element_type=F32)
        for pair in range(PAIRS):
            two = x[2 * VS * pair : 2 * VS * (pair + 1)]
            for q in range(DC // 4):
                v = [two[:, 4 * V * q + PAD * e : 4 * V * q + PAD * (e + 1)] for e in range(3)]
                d = [
                    v[0],
                    jnp.where(lane < 32, pltpu.roll(v[0], 32, 1), pltpu.roll(v[1], 32, 1)),
                    jnp.where(lane < 64, pltpu.roll(v[1], 64, 1), pltpu.roll(v[2], 64, 1)),
                    pltpu.roll(v[2], 96, 1),
                ]
                d = [jnp.concatenate([y[:VS], y[VS:]], 1) for y in d]
                w[PAIRS * m + pair, 4 * VS * q : 4 * VS * (q + 1), :] = jnp.concatenate(d, 0).astype(BF)

    loop(VS // 2 // PAIRS, body)


def ladder(left, w, total):
    for pair in range(VS // 2):
        total[:, 2 * PAD * pair : 2 * PAD * (pair + 1)] += jnp.dot(left(), w[pair], preferred_element_type=F32)


def one_hot(size, outer, inner):
    row = lax.broadcasted_iota(jnp.int32, (size, size), 0)
    col = lax.broadcasted_iota(jnp.int32, (size, size), 1)
    x = lax.shift_right_logical(col, inner.bit_length() - 1)
    y = lax.bitwise_and(col, inner - 1)
    return jnp.where(row == y * outer + x, 1.0, 0.0).astype(BF)


def first_factor(raw, plane, left):
    for h in range(NAUX // PAD):
        lanes = slice(PAD * h, PAD * (h + 1))
        plane[...] = raw[:SLAB, lanes].astype(F32)

        def body(s):
            for a in range(0, VS, 2):
                two = [plane[pl.ds(VS * VS * s + a + e, VS, stride=VS), :] for e in range(2)]
                left[pl.ds(pl.multiple_of(s * (VS * VS) + VS * a, 2 * VS), 2 * VS), lanes] = jnp.concatenate(
                    two, 0
                ).astype(BF)

        loop(4, body)


def flip_factor(raw, plane, ft):
    wide = 4 * V
    for h in range(NAUX // PAD):
        for g in range(SLAB // wide):
            lo = NAUX * g + PAD * h
            plane[wide * g : wide * (g + 1), :] = raw[lo : lo + PAD, :].astype(F32).T

        def body(d):
            two = [plane[pl.ds(2 * d + e, VS, stride=V), :] for e in range(2)]
            ft[rows_of(d, 2 * VS), PAD * h : PAD * (h + 1)] = jnp.concatenate(two, 0).astype(BF)

        loop(V // 2, body)


def flip_pairs(lw, swap, plane, flat):
    wide = 4 * V
    for h in range(OO // PAD):
        rows = slice(PAD * h, PAD * (h + 1))
        for g in range(SLAB // wide):
            x = jnp.dot(swap[rows], lw[:, wide * g : wide * (g + 1)], preferred_element_type=F32)
            plane[wide * g : wide * (g + 1), :] = x.T
        for g in range(V // O):
            x = jnp.concatenate([plane[pl.ds(O * g + d, VS, stride=V), :] for d in range(O)], 0)
            flat[rows, wide * g : wide * (g + 1)] = x.astype(BF).T


def cycle_left(sw, swap, cyc):
    def body(g):
        x = jnp.dot(swap, sw[:, rows_of(g, 4 * V)], preferred_element_type=F32)
        for r in range(4):
            for m in range(4):
                part = [x[O * k : O * (k + 1), V * r : V * (r + 1)] for k in range(4 * m, 4 * m + 4)]
                cyc[pl.ds(pl.multiple_of(g * (4 * O) + O * r, O), O), 4 * V * m : 4 * V * (m + 1)] = jnp.concatenate(
                    part, 1
                ).astype(BF)

    loop(VS // 4, body)


def cycle_right(part, swap, right):
    slabs = [jnp.dot(swap, part(s), preferred_element_type=F32) for s in range(4)]
    for k in range(O):
        right[V * k : V * (k + 1), :] = jnp.concatenate([x[VS * k : VS * (k + 1)] for x in slabs], 0).astype(BF)


G_CHUNKS = 4
SLOTS = 5
GC = O * V // G_CHUNKS


def kernel(
    n, src, lam, chol, g_in, out, fall, gall, z, stage, lw, sw, raw, ft, f, w, lall, total, plane, left, cyc, more,
    cycle, theirs, z_send, z_recv, w_send, w_recv, b_send, b_recv, l_send, l_recv, g_send, g_recv, o_send, o_recv,
    raw_sem, part_sem,
):
    at = Place()
    rows = 2 * OO // n
    lanes = SLAB // 2

    def piece(ref, q):
        return ref.at[rows_of(q // 2, rows), pl.ds(pl.multiple_of((q % 2) * lanes, 128), lanes)]

    chol_in = [
        pltpu.make_async_copy(chol.at[:, pl.ds(NAUX * g, NAUX)], raw.at[pl.ds(NAUX * g, NAUX)], raw_sem.at[g])
        for g in range(SLAB // NAUX)
    ]
    for copy in chol_in:
        copy.start()
    barrier = pltpu.get_barrier_semaphore()

    def greet(o):
        pl.semaphore_signal(barrier, inc=1, device_id=((at.kp + o) % n, 3 - at.y), device_id_type=MESH)

    def greet_plane(o):
        pl.semaphore_signal(barrier, inc=1, device_id=((at.kp + o + 1) % n, at.y), device_id_type=MESH)

    pl.semaphore_signal(barrier, inc=1, device_id=at.cross, device_id_type=MESH)
    loop(n, greet)
    loop(n - 1, greet_plane)
    for copy in chol_in:
        copy.wait()
    flip_factor(raw, plane, ft)

    @pl.when(at.home)
    def _():
        first_factor(ft, plane, left)

    total[...] = jnp.zeros_like(total)
    pl.semaphore_wait(barrier, 2 * n)

    def spread(o):
        q = (at.kp + o + 1) % n
        return remote(piece(lam, q), z.at[at.kp], z_send.at[q], z_recv.at[at.kp], (q, at.y))

    def spread_in(o):
        q = (at.kp + o + 1) % n
        return remote(piece(lam, at.kp), z.at[q], z_send.at[q], z_recv.at[q], (q, at.y))

    z_own = pltpu.make_async_copy(piece(lam, at.kp), z.at[at.kp], z_recv.at[at.kp])

    def place(kind, t):
        e = t % 2
        moved = (e + at.half) % 2
        device = (t + moved * (1 - 2 * e), at.y + moved * (3 - 2 * at.y))
        to = (lw, sw)[kind]
        return remote(stage.at[t], piece(to, at.kp), w_send.at[kind, t], w_recv.at[kind, at.kp], device)

    def place_own(kind):
        return pltpu.make_async_copy(stage.at[at.kp], piece((lw, sw)[kind], at.kp), w_recv.at[kind, at.kp])

    def place_in(kind, q):
        to = (lw, sw)[kind]
        return remote(stage.at[q], piece(to, q), w_send.at[kind, q], w_recv.at[kind, q], at.partner)

    def send_picked(kind):
        def pick(t):
            stage[t] = z[src[kind, t]]

        loop(n, pick)
        loop(n - 1, lambda o: place(kind, (at.kp + o + 1) % n).start())

        @pl.when(at.home)
        def _():
            place_own(kind).start()

        @pl.when(at.away)
        def _():
            place(kind, at.kp).start()

    def sent_picked(kind):
        loop(n - 1, lambda o: place(kind, (at.kp + o + 1) % n).wait_send())

        @pl.when(at.away)
        def _():
            place(kind, at.kp).wait_send()

    def take_picked(kind):
        @pl.when(at.home)
        def _():
            loop(n - 1, lambda o: place_in(kind, (at.kp + o + 1) % n).wait_recv())
            place_own(kind).wait()

        @pl.when(at.away)
        def _():
            loop(n, lambda q: place_in(kind, q).wait_recv())

    def b_copy(kind, src_ref, slab, k, device):
        cut = pl.ds(CROWS * k, CROWS)
        return remote(src_ref.at[cut], fall.at[slab, cut], b_send.at[kind, k], b_recv.at[kind, k], device)

    def l_copy(kind, slab, device):
        return remote(lall.at[slab], lall.at[slab], l_send.at[kind], l_recv.at[kind], device)

    def g_copy(kind, src_ref, slab, j, device):
        cut = pl.ds(GC * j, GC)
        return remote(src_ref.at[:, cut], gall.at[slab, :, cut], g_send.at[kind, j], g_recv.at[kind, j], device)

    def fetch(mine, theirs, to, sem):
        @pl.when(at.home)
        def _():
            pltpu.make_async_copy(mine, to, sem).start()

        @pl.when(at.away)
        def _():
            pltpu.make_async_copy(theirs, to, sem).start()

    def issue(k):
        @pl.when(at.home)
        def _():
            b_copy(1, ft, at.own_slab, k, at.cross).start()
            b_copy(0, ft, at.own_slab, k, at.mate).start()

    def relay(k):
        @pl.when(at.away)
        def _():
            b_copy(3, ft, at.own_slab, k, at.partner).wait_recv()
            b_copy(1, fall.at[at.own_slab], at.own_slab, k, at.cross).start()
            b_copy(0, fall.at[at.own_slab], at.own_slab, k, at.mate).start()

    def swap_factor(k):
        @pl.when(at.away)
        def _():
            b_copy(3, ft, at.y, k, at.partner).start()

    def wait_diag(k):
        b_copy(2, ft, at.diag_slab, k, at.mate).wait_recv()

    def forward(k):
        b_copy(1, ft, at.cross_slab, k, at.cross).wait_recv()
        b_copy(2, fall.at[at.cross_slab], at.cross_slab, k, at.mate).start()

    def send_g(j):
        @pl.when(at.home)
        def _():
            g_copy(1, g_in, at.own_slab, j, at.cross).start()
            g_copy(0, g_in, at.own_slab, j, at.mate).start()

        @pl.when(at.away)
        def _():
            g_copy(3, g_in, at.own_slab, j, at.partner).wait_recv()
            g_copy(1, gall.at[at.own_slab], at.own_slab, j, at.cross).start()
            g_copy(0, gall.at[at.own_slab], at.own_slab, j, at.mate).start()

    def forward_g(j):
        g_copy(1, g_in, at.cross_slab, j, at.cross).wait_recv()
        g_copy(2, gall.at[at.cross_slab], at.cross_slab, j, at.mate).start()

    for k in range(D_CHUNKS):
        issue(k)
        swap_factor(k)
    loop(n - 1, lambda o: spread(o).start())
    z_own.start()
    relay(0)
    forward(0)
    wait_diag(0)
    relay(1)
    loop(n - 1, lambda o: spread_in(o).wait_recv())
    z_own.wait()
    send_picked(0)
    relay(2)

    @pl.when(at.away)
    def _():
        for j in range(G_CHUNKS):
            g_copy(3, g_in, at.y, j, at.partner).start()
        copy = pltpu.make_async_copy(fall.at[at.own_slab], raw.at[pl.ds(0, SLAB)], raw_sem.at[0])
        copy.start()
        copy.wait()
        first_factor(raw, plane, left)

    def prepare(k):
        b_copy(0, ft, at.mate_slab, k, at.mate).wait_recv()
        cut = pl.ds(CROWS * k, CROWS)
        slabs = (at.own_slab, at.mate_slab, at.cross_slab, at.diag_slab)
        copies = [
            pltpu.make_async_copy(fall.at[slab, cut], raw.at[rows_of(slab, CROWS)], raw_sem.at[i])
            for i, slab in enumerate(slabs)
        ]
        fetch(ft.at[cut], fall.at[at.own_slab, cut], raw.at[rows_of(at.own_slab, CROWS)], raw_sem.at[0])
        for copy in copies[1:]:
            copy.start()
        for copy in copies:
            copy.wait()
        merge_factor(raw, f, k)

    def pick_slab(far, e):
        two = (at.cross_slab, at.diag_slab) if far else (at.own_slab, at.mate_slab)
        return two[0] + e * (two[1] - two[0])

    def form_blocks(far, first, count):
        def body(i):
            b = first + i
            slab = pick_slab(far, b % 2)

            def rows(m):
                size = 2 * VS * PAIRS
                return left[rows_of(slab * (VS // 2 // PAIRS) + m, size), :]

            form(rows, f, b // 2, w.at[b % SLOTS])

        loop(count, body)

    def ladder_blocks(far, first, count):
        def body(i):
            b = first + i
            slab = pick_slab(far, b % 2)
            cut = rows_of(b // 2, CROWS)
            ladder(lambda: lall[slab, :, cut], w.at[b % SLOTS], total)

        loop(count, body)

    last = 2 * D_CHUNKS - SLOTS
    prepare(0)
    form_blocks(False, 0, 2)
    forward(1)
    wait_diag(1)
    prepare(1)
    form_blocks(False, 2, 2)
    forward(2)
    send_g(0)
    send_g(1)
    wait_diag(2)
    prepare(2)
    form_blocks(False, 4, SLOTS - 4)
    take_picked(0)
    swap_rows = one_hot(OO, O, O)
    flip_pairs(lw, swap_rows, plane, lall.at[at.own_slab])
    l_copy(1, at.own_slab, at.cross).start()
    l_copy(0, at.own_slab, at.mate).start()
    sent_picked(0)

    send_picked(1)
    l_copy(0, at.mate_slab, at.mate).wait_recv()
    ladder_blocks(False, 0, SLOTS)
    form_blocks(False, SLOTS, last)
    ladder_blocks(False, SLOTS, last)
    form_blocks(True, 0, SLOTS - 2)
    send_g(2)
    send_g(3)
    form_blocks(True, SLOTS - 2, 2)
    take_picked(1)
    cycle_left(sw, one_hot(OO, O, O), cyc)
    l_copy(1, at.cross_slab, at.cross).wait_recv()
    l_copy(2, at.cross_slab, at.mate).start()
    forward_g(0)
    forward_g(1)
    l_copy(2, at.diag_slab, at.mate).wait_recv()
    ladder_blocks(True, 0, SLOTS)

    half = O * V

    def part_of(j):
        return raw.at[pl.ds(half, half)] if j % 2 == 0 else more

    def part_copy(j, i):
        slab = (at.own_slab, at.mate_slab, at.cross_slab, at.diag_slab)[i]
        cols = pl.ds(GC * j, GC)
        to = part_of(j).at[rows_of(slab, VS * O)]
        return pltpu.make_async_copy(gall.at[slab, :, cols], to, part_sem.at[j % 2, i])

    def take_g(j):
        g_copy(0, g_in, at.mate_slab, j, at.mate).wait_recv()
        g_copy(2, g_in, at.diag_slab, j, at.mate).wait_recv()
        cols = pl.ds(GC * j, GC)
        to = part_of(j).at[rows_of(at.own_slab, VS * O)]
        fetch(g_in.at[:, cols], gall.at[at.own_slab, :, cols], to, part_sem.at[j % 2, 0])
        for i in range(1, 4):
            part_copy(j, i).start()

    def o_copy(j):
        cut = pl.ds(4 * O * j, 4 * O)
        return remote(lw.at[cut], theirs.at[cut], o_send.at[j], o_recv.at[j], at.partner)

    def finish(j):
        for i in range(4):
            part_copy(j, i).wait()
        swap = one_hot(VS * O, VS, O)
        cycle_right(lambda s: part_of(j)[VS * O * s : VS * O * (s + 1), :], swap, raw)
        cycle[...] = jnp.dot(cyc[...], raw[:half, :], preferred_element_type=F32)
        def body(m):
            cyc_rows = cycle[rows_of(m, 4 * O), :]
            for r in range(4):
                rows = slice(O * (4 * j + r), O * (4 * j + r + 1))
                lad = total[rows, rows_of(m, 4 * PAD)]
                x = [
                    lad[:, PAD * e : PAD * e + V] + cyc_rows[O * e : O * (e + 1), V * r : V * (r + 1)] for e in range(4)
                ]
                x = jnp.concatenate(x, 1)
                out[rows, rows_of(m, 4 * V)] = x
                lw[rows, rows_of(m, 4 * V)] = x.astype(BF)

        loop(VS // 4, body)

        @pl.when(at.away)
        def _():
            o_copy(j).start()

    take_g(0)
    take_g(1)
    form_blocks(True, SLOTS, last)
    ladder_blocks(True, SLOTS, last)
    finish(0)
    forward_g(2)
    take_g(2)
    finish(1)
    forward_g(3)
    take_g(3)
    finish(2)
    finish(3)

    @pl.when(at.away)
    def _():
        for j in range(G_CHUNKS):
            cut = slice(4 * O * j, 4 * O * (j + 1))
            o_copy(j).wait_recv()
            out[cut, :] = theirs[cut, :].astype(F32)
        for j in range(G_CHUNKS):
            o_copy(j).wait_send()

    loop(n - 1, lambda o: spread(o).wait_send())
    sent_picked(1)

    @pl.when(at.away)
    def _():
        for k in range(D_CHUNKS):
            b_copy(3, ft, at.y, k, at.partner).wait_send()
        for j in range(G_CHUNKS):
            g_copy(3, g_in, at.y, j, at.partner).wait_send()

    for kind in range(3):
        l_copy(kind, at.own_slab, at.mate).wait_send()
        for k in range(D_CHUNKS):
            b_copy(kind, ft, at.own_slab, k, at.mate).wait_send()
        for j in range(G_CHUNKS):
            g_copy(kind, g_in, at.own_slab, j, at.mate).wait_send()


def call(n, sources, lam, chol, g_in):
    anywhere = pl.BlockSpec(memory_space=pl.ANY)
    dma = pltpu.SemaphoreType.DMA
    rows = 2 * OO // n
    out, _, _ = pl.pallas_call(
        functools.partial(kernel, n),
        out_shape=(
            jax.ShapeDtypeStruct((OO, SLAB), F32),
            jax.ShapeDtypeStruct((4, SLAB, NAUX), BF),
            jax.ShapeDtypeStruct((4, VS * O, O * V), BF),
        ),
        in_specs=[pl.BlockSpec(memory_space=pltpu.SMEM)] + [anywhere] * 3,
        out_specs=(pl.BlockSpec(memory_space=pltpu.VMEM), anywhere, anywhere),
        scratch_shapes=[
            pltpu.VMEM((n, rows, SLAB // 2), BF),
            pltpu.VMEM((n, rows, SLAB // 2), BF),
            pltpu.VMEM((OO, SLAB), BF),
            pltpu.VMEM((OO, SLAB), BF),
            pltpu.VMEM((4 * CROWS, NAUX), BF),
            pltpu.VMEM((SLAB, NAUX), BF),
            pltpu.VMEM((NAUX, V * V), BF),
            pltpu.VMEM((SLOTS, VS // 2, CROWS, 2 * PAD), BF),
            pltpu.VMEM((4, OO, SLAB), BF),
            pltpu.VMEM((OO, VS * PAD), F32),
            pltpu.VMEM((SLAB, PAD), F32),
            pltpu.VMEM((SLAB, NAUX), BF),
            pltpu.VMEM((VS * O, O * V), BF),
            pltpu.VMEM((O * V, GC), BF),
            pltpu.VMEM((VS * O, GC), F32),
            pltpu.VMEM((OO, SLAB), BF),
            dma((n,)),
            dma((n,)),
            dma((2, n)),
            dma((2, n)),
            dma((4, D_CHUNKS)),
            dma((4, D_CHUNKS)),
            dma((3,)),
            dma((3,)),
            dma((4, G_CHUNKS)),
            dma((4, G_CHUNKS)),
            dma((G_CHUNKS,)),
            dma((G_CHUNKS,)),
            dma((SLAB // NAUX,)),
            dma((2, 4)),
        ],
        compiler_params=pltpu.CompilerParams(collective_id=0, has_side_effects=True, vmem_limit_bytes=63 << 20),
        name="residual",
    )(jnp.transpose(sources), lam, chol, g_in)
    return out


def local(n, lam, chol, cycle_int, sources):
    out = call(n, sources, lam[0], chol[0], cycle_int[0])
    return jnp.transpose(out.reshape(O, O, SLAB), (1, 0, 2)).reshape(1, OO, SLAB)


def solution(mesh):
    placed = (P("kpair", None, "vir"), P("kpair", None, "vir"), P("kpair", "vir", None), P())
    return jax.shard_map(
        functools.partial(local, mesh.shape["kpair"]),
        mesh=mesh,
        in_specs=placed,
        out_specs=P("kpair", None, "vir"),
        check_vma=False,
    )
```

```python
import functools

import jax
import jax.numpy as jnp
from jax import lax
from jax.experimental import pallas as pl
from jax.experimental.pallas import tpu as pltpu
from jax.sharding import PartitionSpec as P

O = 16
V = 96
VS = 24
NAUX = 384
OO = O * O
SLAB = VS * V
PAD = 128
BF = jnp.bfloat16
F32 = jnp.float32
MESH = pl.DeviceIdType.MESH
D_CHUNKS = 3
DC = V // D_CHUNKS
CROWS = DC * VS


class Place:
    def __init__(self):
        kp = lax.axis_index("kpair")
        y = lax.axis_index("vir")
        core = kp % 2
        half = y // 2
        guest = (core + half) % 2
        other = y + 1 - 2 * (y % 2)
        swap = kp + 1 - 2 * core
        self.kp, self.y, self.half, self.guest = kp, y, half, guest
        self.home = guest == 0
        self.away = guest == 1
        self.mate = (swap, y)
        self.cross = (kp, other)
        self.partner = (swap, 3 - y)
        self.own_slab = y + guest * (3 - 2 * y)
        self.mate_slab = y + (1 - guest) * (3 - 2 * y)
        self.cross_slab = other + guest * (3 - 2 * other)
        self.diag_slab = other + (1 - guest) * (3 - 2 * other)


def remote(src, dst, send, recv, device):
    return pltpu.make_async_remote_copy(
        src_ref=src, dst_ref=dst, send_sem=send, recv_sem=recv, device_id=device, device_id_type=MESH
    )


def loop(count, body):
    def step(i, carry):
        body(i)
        return carry

    lax.fori_loop(0, count, step, 0)


def rows_of(index, size):
    return pl.ds(pl.multiple_of(index * size, size), size)


def merge_factor(raw, f, k):
    def body(g):
        parts = [
            raw[pl.ds(pl.multiple_of(g * (4 * VS) + CROWS * s, 2 * VS), 4 * VS), :].astype(F32) for s in range(4)
        ]
        out = [part[VS * h : VS * (h + 1)] for h in range(4) for part in parts]
        f[:, rows_of(g + k * (DC // 4), 4 * V)] = jnp.concatenate(out, 0).astype(BF).T

    loop(DC // 4, body)


PAIRS = 6


def form(left, f, k, w):
    lane = lax.broadcasted_iota(jnp.int32, (2 * VS, PAD), 1)

    def body(m):
        x = jnp.dot(left(m), f[:, rows_of(k, DC * V)], preferred_element_type=F32)
        for pair in range(PAIRS):
            two = x[2 * VS * pair : 2 * VS * (pair + 1)]
            for q in range(DC // 4):
                v = [two[:, 4 * V * q + PAD * e : 4 * V * q + PAD * (e + 1)] for e in range(3)]
                d = [
                    v[0],
                    jnp.where(lane < 32, pltpu.roll(v[0], 32, 1), pltpu.roll(v[1], 32, 1)),
                    jnp.where(lane < 64, pltpu.roll(v[1], 64, 1), pltpu.roll(v[2], 64, 1)),
                    pltpu.roll(v[2], 96, 1),
                ]
                d = [jnp.concatenate([y[:VS], y[VS:]], 1) for y in d]
                w[PAIRS * m + pair, 4 * VS * q : 4 * VS * (q + 1), :] = jnp.concatenate(d, 0).astype(BF)

    loop(VS // 2 // PAIRS, body)


def ladder(left, w, total):
    for pair in range(VS // 2):
        total[:, 2 * PAD * pair : 2 * PAD * (pair + 1)] += jnp.dot(left(), w[pair], preferred_element_type=F32)


def one_hot(size, outer, inner):
    row = lax.broadcasted_iota(jnp.int32, (size, size), 0)
    col = lax.broadcasted_iota(jnp.int32, (size, size), 1)
    x = lax.shift_right_logical(col, inner.bit_length() - 1)
    y = lax.bitwise_and(col, inner - 1)
    return jnp.where(row == y * outer + x, 1.0, 0.0).astype(BF)


def first_factor(raw, plane, left):
    for h in range(NAUX // PAD):
        lanes = slice(PAD * h, PAD * (h + 1))
        plane[...] = raw[:SLAB, lanes].astype(F32)

        def body(s):
            for a in range(0, VS, 2):
                two = [plane[pl.ds(VS * VS * s + a + e, VS, stride=VS), :] for e in range(2)]
                left[pl.ds(pl.multiple_of(s * (VS * VS) + VS * a, 2 * VS), 2 * VS), lanes] = jnp.concatenate(
                    two, 0
                ).astype(BF)

        loop(4, body)


def flip_factor(raw, plane, ft):
    wide = 4 * V
    for h in range(NAUX // PAD):
        for g in range(SLAB // wide):
            lo = NAUX * g + PAD * h
            plane[wide * g : wide * (g + 1), :] = raw[lo : lo + PAD, :].astype(F32).T

        def body(d):
            two = [plane[pl.ds(2 * d + e, VS, stride=V), :] for e in range(2)]
            ft[rows_of(d, 2 * VS), PAD * h : PAD * (h + 1)] = jnp.concatenate(two, 0).astype(BF)

        loop(V // 2, body)


def flip_pairs(lw, swap, plane, flat):
    wide = 4 * V
    for h in range(OO // PAD):
        rows = slice(PAD * h, PAD * (h + 1))
        for g in range(SLAB // wide):
            x = jnp.dot(swap[rows], lw[:, wide * g : wide * (g + 1)], preferred_element_type=F32)
            plane[wide * g : wide * (g + 1), :] = x.T
        for g in range(V // O):
            x = jnp.concatenate([plane[pl.ds(O * g + d, VS, stride=V), :] for d in range(O)], 0)
            flat[rows, wide * g : wide * (g + 1)] = x.astype(BF).T


def cycle_left(sw, swap, cyc):
    def body(g):
        x = jnp.dot(swap, sw[:, rows_of(g, 4 * V)], preferred_element_type=F32)
        for r in range(4):
            for m in range(4):
                part = [x[O * k : O * (k + 1), V * r : V * (r + 1)] for k in range(4 * m, 4 * m + 4)]
                cyc[pl.ds(pl.multiple_of(g * (4 * O) + O * r, O), O), 4 * V * m : 4 * V * (m + 1)] = jnp.concatenate(
                    part, 1
                ).astype(BF)

    loop(VS // 4, body)


def cycle_right(part, swap, right):
    slabs = [jnp.dot(swap, part(s), preferred_element_type=F32) for s in range(4)]
    for k in range(O):
        right[V * k : V * (k + 1), :] = jnp.concatenate([x[VS * k : VS * (k + 1)] for x in slabs], 0).astype(BF)


G_CHUNKS = 4
SLOTS = 5
GC = O * V // G_CHUNKS


def kernel(
    n, src, lam, chol, g_in, out, fall, gall, z, stage, lw, sw, raw, ft, f, w, lall, total, plane, left, cyc, more,
    cycle, theirs, z_send, z_recv, w_send, w_recv, b_send, b_recv, l_send, l_recv, g_send, g_recv, o_send, o_recv,
    raw_sem, part_sem,
):
    at = Place()
    rows = 2 * OO // n
    lanes = SLAB // 2

    def piece(ref, q):
        return ref.at[rows_of(q // 2, rows), pl.ds(pl.multiple_of((q % 2) * lanes, 128), lanes)]

    chol_in = [
        pltpu.make_async_copy(chol.at[:, pl.ds(NAUX * g, NAUX)], raw.at[pl.ds(NAUX * g, NAUX)], raw_sem.at[g])
        for g in range(SLAB // NAUX)
    ]
    for copy in chol_in:
        copy.start()
    barrier = pltpu.get_barrier_semaphore()

    def greet(o):
        pl.semaphore_signal(barrier, inc=1, device_id=((at.kp + o) % n, 3 - at.y), device_id_type=MESH)

    def greet_plane(o):
        pl.semaphore_signal(barrier, inc=1, device_id=((at.kp + o + 1) % n, at.y), device_id_type=MESH)

    pl.semaphore_signal(barrier, inc=1, device_id=at.cross, device_id_type=MESH)
    loop(n, greet)
    loop(n - 1, greet_plane)
    for copy in chol_in:
        copy.wait()
    flip_factor(raw, plane, ft)

    @pl.when(at.home)
    def _():
        first_factor(ft, plane, left)

    total[...] = jnp.zeros_like(total)
    pl.semaphore_wait(barrier, 2 * n)

    def spread(o):
        q = (at.kp + o + 1) % n
        return remote(piece(lam, q), z.at[at.kp], z_send.at[q], z_recv.at[at.kp], (q, at.y))

    def spread_in(o):
        q = (at.kp + o + 1) % n
        return remote(piece(lam, at.kp), z.at[q], z_send.at[q], z_recv.at[q], (q, at.y))

    z_own = pltpu.make_async_copy(piece(lam, at.kp), z.at[at.kp], z_recv.at[at.kp])

    def place(kind, t):
        e = t % 2
        moved = (e + at.half) % 2
        device = (t + moved * (1 - 2 * e), at.y + moved * (3 - 2 * at.y))
        to = (lw, sw)[kind]
        return remote(stage.at[t], piece(to, at.kp), w_send.at[kind, t], w_recv.at[kind, at.kp], device)

    def place_own(kind):
        return pltpu.make_async_copy(stage.at[at.kp], piece((lw, sw)[kind], at.kp), w_recv.at[kind, at.kp])

    def place_in(kind, q):
        to = (lw, sw)[kind]
        return remote(stage.at[q], piece(to, q), w_send.at[kind, q], w_recv.at[kind, q], at.partner)

    def send_picked(kind):
        def pick(t):
            stage[t] = z[src[kind, t]]

        loop(n, pick)
        loop(n - 1, lambda o: place(kind, (at.kp + o + 1) % n).start())

        @pl.when(at.home)
        def _():
            place_own(kind).start()

        @pl.when(at.away)
        def _():
            place(kind, at.kp).start()

    def sent_picked(kind):
        loop(n - 1, lambda o: place(kind, (at.kp + o + 1) % n).wait_send())

        @pl.when(at.away)
        def _():
            place(kind, at.kp).wait_send()

    def take_picked(kind):
        @pl.when(at.home)
        def _():
            loop(n - 1, lambda o: place_in(kind, (at.kp + o + 1) % n).wait_recv())
            place_own(kind).wait()

        @pl.when(at.away)
        def _():
            loop(n, lambda q: place_in(kind, q).wait_recv())

    def b_copy(kind, src_ref, slab, k, device):
        cut = pl.ds(CROWS * k, CROWS)
        return remote(src_ref.at[cut], fall.at[slab, cut], b_send.at[kind, k], b_recv.at[kind, k], device)

    def l_copy(kind, slab, device):
        return remote(lall.at[slab], lall.at[slab], l_send.at[kind], l_recv.at[kind], device)

    def g_copy(kind, src_ref, slab, j, device):
        cut = pl.ds(GC * j, GC)
        return remote(src_ref.at[:, cut], gall.at[slab, :, cut], g_send.at[kind, j], g_recv.at[kind, j], device)

    def fetch(mine, theirs, to, sem):
        @pl.when(at.home)
        def _():
            pltpu.make_async_copy(mine, to, sem).start()

        @pl.when(at.away)
        def _():
            pltpu.make_async_copy(theirs, to, sem).start()

    def issue(k):
        @pl.when(at.home)
        def _():
            b_copy(1, ft, at.own_slab, k, at.cross).start()
            b_copy(0, ft, at.own_slab, k, at.mate).start()

    def relay(k):
        @pl.when(at.away)
        def _():
            b_copy(3, ft, at.own_slab, k, at.partner).wait_recv()
            b_copy(1, fall.at[at.own_slab], at.own_slab, k, at.cross).start()
            b_copy(0, fall.at[at.own_slab], at.own_slab, k, at.mate).start()

    def swap_factor(k):
        @pl.when(at.away)
        def _():
            b_copy(3, ft, at.y, k, at.partner).start()

    def wait_diag(k):
        b_copy(2, ft, at.diag_slab, k, at.mate).wait_recv()

    def forward(k):
        b_copy(1, ft, at.cross_slab, k, at.cross).wait_recv()
        b_copy(2, fall.at[at.cross_slab], at.cross_slab, k, at.mate).start()

    def send_g(j):
        @pl.when(at.home)
        def _():
            g_copy(1, g_in, at.own_slab, j, at.cross).start()
            g_copy(0, g_in, at.own_slab, j, at.mate).start()

        @pl.when(at.away)
        def _():
            g_copy(3, g_in, at.own_slab, j, at.partner).wait_recv()
            g_copy(1, gall.at[at.own_slab], at.own_slab, j, at.cross).start()
            g_copy(0, gall.at[at.own_slab], at.own_slab, j, at.mate).start()

    def forward_g(j):
        g_copy(1, g_in, at.cross_slab, j, at.cross).wait_recv()
        g_copy(2, gall.at[at.cross_slab], at.cross_slab, j, at.mate).start()

    for k in range(D_CHUNKS):
        issue(k)
        swap_factor(k)
    loop(n - 1, lambda o: spread(o).start())
    z_own.start()
    relay(0)
    forward(0)
    wait_diag(0)
    relay(1)
    loop(n - 1, lambda o: spread_in(o).wait_recv())
    z_own.wait()
    send_picked(0)
    relay(2)

    @pl.when(at.away)
    def _():
        for j in range(G_CHUNKS):
            g_copy(3, g_in, at.y, j, at.partner).start()
        copy = pltpu.make_async_copy(fall.at[at.own_slab], raw.at[pl.ds(0, SLAB)], raw_sem.at[0])
        copy.start()
        copy.wait()
        first_factor(raw, plane, left)

    def prepare(k):
        b_copy(0, ft, at.mate_slab, k, at.mate).wait_recv()
        cut = pl.ds(CROWS * k, CROWS)
        slabs = (at.own_slab, at.mate_slab, at.cross_slab, at.diag_slab)
        copies = [
            pltpu.make_async_copy(fall.at[slab, cut], raw.at[rows_of(slab, CROWS)], raw_sem.at[i])
            for i, slab in enumerate(slabs)
        ]
        fetch(ft.at[cut], fall.at[at.own_slab, cut], raw.at[rows_of(at.own_slab, CROWS)], raw_sem.at[0])
        for copy in copies[1:]:
            copy.start()
        for copy in copies:
            copy.wait()
        merge_factor(raw, f, k)

    def pick_slab(far, e):
        two = (at.cross_slab, at.diag_slab) if far else (at.own_slab, at.mate_slab)
        return two[0] + e * (two[1] - two[0])

    def form_blocks(far, first, count):
        def body(i):
            b = first + i
            slab = pick_slab(far, b % 2)

            def rows(m):
                size = 2 * VS * PAIRS
                return left[rows_of(slab * (VS // 2 // PAIRS) + m, size), :]

            form(rows, f, b // 2, w.at[b % SLOTS])

        loop(count, body)

    def ladder_blocks(far, first, count):
        def body(i):
            b = first + i
            slab = pick_slab(far, b % 2)
            cut = rows_of(b // 2, CROWS)
            ladder(lambda: lall[slab, :, cut], w.at[b % SLOTS], total)

        loop(count, body)

    last = 2 * D_CHUNKS - SLOTS
    prepare(0)
    form_blocks(False, 0, 2)
    forward(1)
    wait_diag(1)
    prepare(1)
    form_blocks(False, 2, 2)
    forward(2)
    take_picked(0)
    swap_rows = one_hot(OO, O, O)
    flip_pairs(lw, swap_rows, plane, lall.at[at.own_slab])
    l_copy(1, at.own_slab, at.cross).start()
    l_copy(0, at.own_slab, at.mate).start()
    sent_picked(0)

    send_picked(1)
    send_g(0)
    send_g(1)
    wait_diag(2)
    prepare(2)
    form_blocks(False, 4, SLOTS - 4)
    l_copy(0, at.mate_slab, at.mate).wait_recv()
    ladder_blocks(False, 0, SLOTS)
    form_blocks(False, SLOTS, last)
    ladder_blocks(False, SLOTS, last)
    form_blocks(True, 0, SLOTS - 2)
    send_g(2)
    send_g(3)
    form_blocks(True, SLOTS - 2, 2)
    take_picked(1)
    cycle_left(sw, one_hot(OO, O, O), cyc)
    l_copy(1, at.cross_slab, at.cross).wait_recv()
    l_copy(2, at.cross_slab, at.mate).start()
    forward_g(0)
    forward_g(1)
    l_copy(2, at.diag_slab, at.mate).wait_recv()
    ladder_blocks(True, 0, SLOTS)

    half = O * V

    def part_of(j):
        return raw.at[pl.ds(half, half)] if j % 2 == 0 else more

    def part_copy(j, i):
        slab = (at.own_slab, at.mate_slab, at.cross_slab, at.diag_slab)[i]
        cols = pl.ds(GC * j, GC)
        to = part_of(j).at[rows_of(slab, VS * O)]
        return pltpu.make_async_copy(gall.at[slab, :, cols], to, part_sem.at[j % 2, i])

    def take_g(j):
        g_copy(0, g_in, at.mate_slab, j, at.mate).wait_recv()
        g_copy(2, g_in, at.diag_slab, j, at.mate).wait_recv()
        cols = pl.ds(GC * j, GC)
        to = part_of(j).at[rows_of(at.own_slab, VS * O)]
        fetch(g_in.at[:, cols], gall.at[at.own_slab, :, cols], to, part_sem.at[j % 2, 0])
        for i in range(1, 4):
            part_copy(j, i).start()

    def o_copy(j):
        cut = pl.ds(4 * O * j, 4 * O)
        return remote(lw.at[cut], theirs.at[cut], o_send.at[j], o_recv.at[j], at.partner)

    def finish(j):
        for i in range(4):
            part_copy(j, i).wait()
        swap = one_hot(VS * O, VS, O)
        cycle_right(lambda s: part_of(j)[VS * O * s : VS * O * (s + 1), :], swap, raw)
        cycle[...] = jnp.dot(cyc[...], raw[:half, :], preferred_element_type=F32)
        def body(m):
            cyc_rows = cycle[rows_of(m, 4 * O), :]
            for r in range(4):
                rows = slice(O * (4 * j + r), O * (4 * j + r + 1))
                lad = total[rows, rows_of(m, 4 * PAD)]
                x = [
                    lad[:, PAD * e : PAD * e + V] + cyc_rows[O * e : O * (e + 1), V * r : V * (r + 1)] for e in range(4)
                ]
                x = jnp.concatenate(x, 1)
                out[rows, rows_of(m, 4 * V)] = x
                lw[rows, rows_of(m, 4 * V)] = x.astype(BF)

        loop(VS // 4, body)

        @pl.when(at.away)
        def _():
            o_copy(j).start()

    take_g(0)
    take_g(1)
    form_blocks(True, SLOTS, last)
    ladder_blocks(True, SLOTS, last)
    finish(0)
    forward_g(2)
    take_g(2)
    finish(1)
    forward_g(3)
    take_g(3)
    finish(2)
    finish(3)

    @pl.when(at.away)
    def _():
        for j in range(G_CHUNKS):
            cut = slice(4 * O * j, 4 * O * (j + 1))
            o_copy(j).wait_recv()
            out[cut, :] = theirs[cut, :].astype(F32)
        for j in range(G_CHUNKS):
            o_copy(j).wait_send()

    loop(n - 1, lambda o: spread(o).wait_send())
    sent_picked(1)

    @pl.when(at.away)
    def _():
        for k in range(D_CHUNKS):
            b_copy(3, ft, at.y, k, at.partner).wait_send()
        for j in range(G_CHUNKS):
            g_copy(3, g_in, at.y, j, at.partner).wait_send()

    for kind in range(3):
        l_copy(kind, at.own_slab, at.mate).wait_send()
        for k in range(D_CHUNKS):
            b_copy(kind, ft, at.own_slab, k, at.mate).wait_send()
        for j in range(G_CHUNKS):
            g_copy(kind, g_in, at.own_slab, j, at.mate).wait_send()


def call(n, sources, lam, chol, g_in):
    anywhere = pl.BlockSpec(memory_space=pl.ANY)
    dma = pltpu.SemaphoreType.DMA
    rows = 2 * OO // n
    out, _, _ = pl.pallas_call(
        functools.partial(kernel, n),
        out_shape=(
            jax.ShapeDtypeStruct((OO, SLAB), F32),
            jax.ShapeDtypeStruct((4, SLAB, NAUX), BF),
            jax.ShapeDtypeStruct((4, VS * O, O * V), BF),
        ),
        in_specs=[pl.BlockSpec(memory_space=pltpu.SMEM)] + [anywhere] * 3,
        out_specs=(pl.BlockSpec(memory_space=pltpu.VMEM), anywhere, anywhere),
        scratch_shapes=[
            pltpu.VMEM((n, rows, SLAB // 2), BF),
            pltpu.VMEM((n, rows, SLAB // 2), BF),
            pltpu.VMEM((OO, SLAB), BF),
            pltpu.VMEM((OO, SLAB), BF),
            pltpu.VMEM((4 * CROWS, NAUX), BF),
            pltpu.VMEM((SLAB, NAUX), BF),
            pltpu.VMEM((NAUX, V * V), BF),
            pltpu.VMEM((SLOTS, VS // 2, CROWS, 2 * PAD), BF),
            pltpu.VMEM((4, OO, SLAB), BF),
            pltpu.VMEM((OO, VS * PAD), F32),
            pltpu.VMEM((SLAB, PAD), F32),
            pltpu.VMEM((SLAB, NAUX), BF),
            pltpu.VMEM((VS * O, O * V), BF),
            pltpu.VMEM((O * V, GC), BF),
            pltpu.VMEM((VS * O, GC), F32),
            pltpu.VMEM((OO, SLAB), BF),
            dma((n,)),
            dma((n,)),
            dma((2, n)),
            dma((2, n)),
            dma((4, D_CHUNKS)),
            dma((4, D_CHUNKS)),
            dma((3,)),
            dma((3,)),
            dma((4, G_CHUNKS)),
            dma((4, G_CHUNKS)),
            dma((G_CHUNKS,)),
            dma((G_CHUNKS,)),
            dma((SLAB // NAUX,)),
            dma((2, 4)),
        ],
        compiler_params=pltpu.CompilerParams(collective_id=0, has_side_effects=True, vmem_limit_bytes=63 << 20),
        name="residual",
    )(jnp.transpose(sources), lam, chol, g_in)
    return out


def local(n, lam, chol, cycle_int, sources):
    out = call(n, sources, lam[0], chol[0], cycle_int[0])
    return jnp.transpose(out.reshape(O, O, SLAB), (1, 0, 2)).reshape(1, OO, SLAB)


def solution(mesh):
    placed = (P("kpair", None, "vir"), P("kpair", None, "vir"), P("kpair", "vir", None), P())
    return jax.shard_map(
        functools.partial(local, mesh.shape["kpair"]),
        mesh=mesh,
        in_specs=placed,
        out_specs=P("kpair", None, "vir"),
        check_vma=False,
    )
```
